128 devices in a mesh: slab: 4 (over x_lo, core), brick: 32 (over z, y, x_hi).
Axes of the slice: x: 4 (x_hi: 2, x_lo: 2; x = x_hi * 2 + x_lo), y: 4, z: 4, core: 2. Of those that a mesh axis runs over, the one named last changes fastest.
Arguments:
- positions: float32 [3, 4, 32, 128], P(None, 'slab', 'brick'), may hold values from 0 to 56, as said below
- species: int32 [4, 32, 128], P('slab', 'brick'), may hold values from 0 to 4
- export_index: int32 [4, 32, 128], P('slab', 'brick'), may hold values from 0 to 127
- edge_center: int32 [4, 32, 256], P('slab', 'brick'), may hold values from 0 to 127
- edge_neighbor: int32 [4, 32, 256], P('slab', 'brick'), may hold values from 0 to 1279
- edge_count: int32 [4, 32], P('slab', 'brick'), may hold values from 64 to 256, as said below
- force_target: float32 [3, 4, 32, 128], P(None, 'slab', 'brick'), may hold values from -6 to 6
- radial_weight: float32 [8, 512], replicated, may hold values from -2 to 2
- center_embed: float32 [5, 512], replicated, may hold values from -6 to 6
- neighbor_embed: float32 [5, 512], replicated, may hold values from -6 to 6
- environment_weight: float32 [2, 512, 64], replicated, may hold values from -0.25 to 0.25
- latent_weight: float32 [2, 576, 512], replicated, may hold values from -0.25 to 0.25
- output_weight: float32 [512], replicated, may hold values from -0.25 to 0.25
Outputs:
- forces: float32 [3, 4, 32, 128], P(None, 'slab', 'brick')
- grad_radial: float32 [8, 512], replicated
- grad_center: float32 [5, 512], replicated
- grad_neighbor: float32 [5, 512], replicated
- grad_environment: float32 [2, 512, 64], replicated
- grad_latent: float32 [2, 576, 512], replicated
- grad_output: float32 [512], replicated
The draws below stay inside these ranges and needn't reach their ends.
Inputs may be any that keep to these rules, and one draw needn't show every extreme that they name: `positions`: atom of domain (s, b) has first coordinate in [0, 1.75), second in [1.75 b, 1.75 (b + 1)), third in [1.75 s, 1.75 (s + 1)). `edge_count`: one domain has all 256 slots live in every draw.
All inputs are finite; a program needn't handle non-finite values.
Results may differ from the reference program's by a relative error of at most 0.0003.
Values sent between devices are 32-bit elements; how exact they have to be, the bound alone decides.
A program may use at most 64 MiB of HBM per device.

```python
import math
import jax
import jax.numpy as jnp
from jax import lax

H = 512
M = 64
NB = 8
NS = 5
LAYERS = 2
ATOM_DEV = 128
GHOST = 128
EDGE_DEV = 256
N_SLAB = 4
N_BRICK = 32


cell_width = 1.75


def draw_positions(key, part):
    key = jax.random.fold_in(key, 3)
    fraction = jax.random.uniform(key, (3, N_SLAB, N_BRICK, ATOM_DEV), jnp.float32)
    slab_ids = jnp.arange(N_SLAB, dtype=jnp.float32)[:, None, None]
    brick_ids = jnp.arange(N_BRICK, dtype=jnp.float32)[None, :, None]
    first = fraction[0] * cell_width
    second = (brick_ids + fraction[1]) * cell_width
    third = (slab_ids + fraction[2]) * cell_width
    return jnp.stack([first, second, third], axis=0).astype(jnp.float32)


def draw_edge_count(key, part):
    key = jax.random.fold_in(key, 5)
    first_key, second_key = jax.random.split(key)
    domains = N_SLAB * N_BRICK
    counts = jax.random.randint(first_key, (domains,), EDGE_DEV // 4, EDGE_DEV + 1)
    fullest = jax.random.randint(second_key, (), 0, domains)
    counts = jnp.where(jnp.arange(domains) == fullest, EDGE_DEV, counts)
    return counts.reshape(N_SLAB, N_BRICK).astype(jnp.int32)


def with_ends(result, key, low, high):
    longest = result.shape.index(max(result.shape))
    spots = []
    for shift in (0, 1):
        where = [jax.random.randint(jax.random.fold_in(key, axis), (), 0, length) for axis, length in enumerate(result.shape)]
        where[longest] = (where[longest] + shift) % result.shape[longest]
        spots.append(tuple(where))
    return result.at[spots[0]].set(low).at[spots[1]].set(high)


def block_levels(stream_key, shape, cuts, smallest, largest):
    def one(axis_at, parts):
        draws = jax.random.uniform(jax.random.fold_in(jax.random.fold_in(stream_key, 6), axis_at), (parts,), jnp.float32, smallest / len(cuts), largest / len(cuts))
        return jnp.repeat(jnp.exp(draws), shape[axis_at] // parts).reshape((-1,) + (1,) * (len(shape) - axis_at - 1))

    level = one(*cuts[0])
    for cut in cuts[1:]:
        level = level * one(*cut)
    return level


def gaussian(stream_key, shape, scale, bound, shards=(), held_as=jnp.bfloat16):
    gain = block_levels(stream_key, shape, shards, -0.22, 0.18) if shards else 1.0
    values = jax.random.normal(stream_key, shape, jnp.float32) * scale * gain
    return jnp.minimum(jnp.maximum(values, -bound), bound).astype(held_as)


def setup_inputs(seed: int = 0) -> dict:
    arg_keys = jax.random.split(jax.random.key(seed), 14)
    positions = draw_positions(jax.random.fold_in(arg_keys[13], 71), 0)
    species = with_ends(jax.random.randint(arg_keys[1], (N_SLAB, N_BRICK, ATOM_DEV), 0, NS), jax.random.fold_in(arg_keys[1], 1), 0, NS - 1).astype(jnp.int32)
    export_index = with_ends(jax.random.randint(arg_keys[2], (N_SLAB, N_BRICK, GHOST), 0, ATOM_DEV), jax.random.fold_in(arg_keys[2], 1), 0, ATOM_DEV - 1).astype(jnp.int32)
    edge_center = with_ends(jax.random.randint(arg_keys[3], (N_SLAB, N_BRICK, EDGE_DEV), 0, ATOM_DEV), jax.random.fold_in(arg_keys[3], 1), 0, ATOM_DEV - 1).astype(jnp.int32)
    edge_neighbor = with_ends(jax.random.randint(arg_keys[4], (N_SLAB, N_BRICK, EDGE_DEV), 0, ATOM_DEV + 9 * GHOST), jax.random.fold_in(arg_keys[4], 1), 0, (ATOM_DEV + 9 * GHOST) - 1).astype(jnp.int32)
    edge_count = draw_edge_count(jax.random.fold_in(arg_keys[13], 71), 0)
    force_target = gaussian(arg_keys[6], (3, N_SLAB, N_BRICK, ATOM_DEV), 1.0, 6.0, ((1, 4), (2, 32)), jnp.float32)
    radial_weight = gaussian(arg_keys[7], (NB, H), NB ** -0.5, 2.0, (), jnp.float32)
    center_embed = gaussian(arg_keys[8], (NS, H), 1.0, 6.0, (), jnp.float32)
    neighbor_embed = gaussian(arg_keys[9], (NS, H), 1.0, 6.0, (), jnp.float32)
    environment_weight = gaussian(arg_keys[10], (LAYERS, H, M), H ** -0.5, 0.25, (), jnp.float32)
    latent_weight = gaussian(arg_keys[11], (LAYERS, H + M, H), (H + M) ** -0.5, 0.25, (), jnp.float32)
    output_weight = gaussian(arg_keys[12], (H,), H ** -0.5, 0.25, (), jnp.float32)
    return dict(positions=positions, species=species, export_index=export_index, edge_center=edge_center, edge_neighbor=edge_neighbor, edge_count=edge_count, force_target=force_target, radial_weight=radial_weight, center_embed=center_embed, neighbor_embed=neighbor_embed, environment_weight=environment_weight, latent_weight=latent_weight, output_weight=output_weight)


cell_width = 1.75
cutoff_radius = 6.0
softening = 0.25

def product(left, right):
    return jnp.dot(left, right, precision=lax.Precision.HIGHEST, preferred_element_type=jnp.float32)

def species_onehot(values, count):
    return (values[None, :] == jnp.arange(count, dtype=jnp.int32)[:, None]).astype(jnp.float32)

def edge_energy(params, table_pos, table_hot, center, neighbor, live, atom_count):
    radial_weight, center_embed, neighbor_embed, environment_weight, latent_weight, output_weight = params
    hidden_width = radial_weight.shape[1]
    multiplicity = environment_weight.shape[2]
    edge_slots = center.shape[0]
    vectors = table_pos[:, neighbor] - table_pos[:, center]
    squared = lax.optimization_barrier(jnp.sum(vectors * vectors, axis=0)) + softening
    distance = jnp.sqrt(squared)
    envelope = (1.0 - squared / (cutoff_radius * cutoff_radius)) ** 2 * live
    directions = vectors / distance[None, :]
    orders = jnp.arange(1, radial_weight.shape[0] + 1, dtype=jnp.float32)
    basis = jnp.sin(orders[:, None] * (math.pi / cutoff_radius) * distance[None, :]) / distance[None, :]
    atom_hot = (center[None, :] == jnp.arange(atom_count, dtype=jnp.int32)[:, None]).astype(jnp.float32)
    latent = jax.nn.silu(product(radial_weight.T, basis) + product(center_embed.T, table_hot[:, center]) + product(neighbor_embed.T, table_hot[:, neighbor]))
    for layer_index in range(environment_weight.shape[0]):
        weights = product(environment_weight[layer_index].T, latent) * envelope[None, :]
        tensors = (directions[:, None, :] * weights[None, :, :]).reshape(3 * multiplicity, edge_slots)
        summed = product(tensors, atom_hot.T)
        spread = product(summed, atom_hot)
        invariant = lax.optimization_barrier(jnp.sum((tensors * spread).reshape(3, multiplicity, edge_slots), axis=0))
        update = product(latent_weight[layer_index][:hidden_width].T, latent) + product(latent_weight[layer_index][hidden_width:].T, invariant)
        latent = latent + jax.nn.silu(update)
    return jnp.sum(product(output_weight[None, :], latent)[0] * envelope)

def surround(values, with_shift):
    channels = values.shape[0]
    ghost_count = values.shape[3]
    slab_ids = jnp.arange(N_SLAB, dtype=jnp.int32)
    brick_ids = jnp.arange(N_BRICK, dtype=jnp.int32)
    blocks = []
    for row in range(3):
        for column in range(3):
            block = jnp.roll(values, (1 - row, 1 - column), axis=(1, 2))
            if with_shift:
                cross_z = ((slab_ids + row - 1 + N_SLAB) // N_SLAB - 1).astype(jnp.float32) * (N_SLAB * cell_width)
                cross_y = ((brick_ids + column - 1 + N_BRICK) // N_BRICK - 1).astype(jnp.float32) * (N_BRICK * cell_width)
                block = block.at[2].add(jnp.broadcast_to(cross_z[:, None, None], block.shape[1:]))
                block = block.at[1].add(jnp.broadcast_to(cross_y[None, :, None], block.shape[1:]))
            blocks.append(block)
    stacked = jnp.stack(blocks, axis=3)
    return jnp.transpose(stacked, (1, 2, 0, 3, 4)).reshape(N_SLAB * N_BRICK, channels, 9 * ghost_count)

def reference(positions, species, export_index, edge_center, edge_neighbor, edge_count, force_target, radial_weight, center_embed, neighbor_embed, environment_weight, latent_weight, output_weight):
    params = (radial_weight, center_embed, neighbor_embed, environment_weight, latent_weight, output_weight)
    atom_count = positions.shape[3]
    ghost_count = export_index.shape[2]
    edge_slots = edge_center.shape[2]
    species_count = center_embed.shape[0]
    domains = N_SLAB * N_BRICK
    exported_pos = jnp.take_along_axis(positions, export_index[None], axis=3)
    exported_species = jnp.take_along_axis(species, export_index, axis=2)
    own_pos = jnp.transpose(positions, (1, 2, 0, 3)).reshape(domains, 3, atom_count)
    table_pos = jnp.concatenate([own_pos, surround(exported_pos, True)], axis=2)
    ghost_species = surround(exported_species[None], False)[:, 0]
    table_species = jnp.concatenate([species.reshape(domains, atom_count), ghost_species], axis=1)
    centers = edge_center.reshape(domains, edge_slots)
    neighbors = edge_neighbor.reshape(domains, edge_slots)
    live = (jnp.arange(edge_slots, dtype=jnp.int32)[None, :] < edge_count.reshape(domains, 1)).astype(jnp.float32)

    def position_gradient(inputs):
        tpos, tspecies, center, neighbor, alive = inputs
        return jax.grad(edge_energy, argnums=1)(params, tpos, species_onehot(tspecies, species_count), center, neighbor, alive, atom_count)
    gradients = lax.map(position_gradient, (table_pos, table_species, centers, neighbors, live))
    own_grad = gradients[:, :, :atom_count]
    ghost_grad = gradients[:, :, atom_count:].reshape(N_SLAB, N_BRICK, 3, 3, 3, ghost_count)
    ghost_grad = jnp.transpose(ghost_grad, (3, 4, 2, 0, 1, 5))
    returned = jnp.zeros((3, N_SLAB, N_BRICK, ghost_count), jnp.float32)
    for row in range(3):
        for column in range(3):
            returned = returned + jnp.roll(ghost_grad[row, column], (row - 1, column - 1), axis=(1, 2))
    returned = jnp.transpose(returned, (1, 2, 0, 3)).reshape(domains, 3, ghost_count)
    exports = export_index.reshape(domains, ghost_count)
    total = jax.vmap(lambda own, index, back: own.at[:, index].add(back))(own_grad, exports, returned)
    forces = -jnp.transpose(total.reshape(N_SLAB, N_BRICK, 3, atom_count), (2, 0, 1, 3))
    cotangent = 2.0 * (forces - force_target) / (3.0 * atom_count)
    exported_tangent = jnp.take_along_axis(cotangent, export_index[None], axis=3)
    own_tangent = jnp.transpose(cotangent, (1, 2, 0, 3)).reshape(domains, 3, atom_count)
    table_tangent = jnp.concatenate([own_tangent, surround(exported_tangent, False)], axis=2)

    def accumulate(carry, inputs):
        tpos, ttangent, tspecies, center, neighbor, alive = inputs
        table_hot = species_onehot(tspecies, species_count)

        def param_gradient(position_table):
            return jax.grad(edge_energy, argnums=0)(params, position_table, table_hot, center, neighbor, alive, atom_count)
        unused, tangents = jax.jvp(param_gradient, (tpos,), (ttangent,))
        return (jax.tree.map(lambda left, right: left + right, carry, tangents), None)
    start = jax.tree.map(lambda value: jnp.zeros(value.shape, jnp.float32), params)
    summed, unused = lax.scan(accumulate, start, (table_pos, table_tangent, table_species, centers, neighbors, live))
    grads = jax.tree.map(lambda value: -value, summed)
    return (forces, grads[0], grads[1], grads[2], grads[3], grads[4], grads[5])
```

```python
import math

import jax
import jax.numpy as jnp
from jax import lax
from jax.experimental import pallas as pl
from jax.experimental.pallas import tpu as pltpu
from jax.sharding import PartitionSpec as P

F32 = jnp.float32
BF16 = jnp.bfloat16
MESH = pl.DeviceIdType.MESH
VMEM = pltpu.VMEM
NN = (((1,), (0,)), ((), ()))
NT = (((1,), (1,)), ((), ()))
TN = (((0,), (0,)), ((), ()))

cell_width = 1.75
cutoff_radius = 6.0
softening = 0.25

N_SLAB, N_BRICK = 4, 32
H, M, E, ATOMS = 512, 64, 256, 128
ROWS = (576, 768)
PARTS = ((192, 192, 192), (256, 256, 256))
ORDERS = (("x", "y", "z"), ("y", "z", "x"), ("z", "x", "y"))
NEIGHBOURS = [(p, q) for p in range(3) for q in range(3) if (p, q) != (1, 1)]


def dot(a, b, dims=NN):
    return lax.dot_general(a, b, dims, preferred_element_type=F32)


def split(x):
    high = x.astype(BF16)
    return high, (x - high.astype(F32)).astype(BF16)


def mm3(a, b, dims=NN):
    return dot(a[0], b[0], dims) + (dot(a[0], b[1], dims) + dot(a[1], b[0], dims))


def mm2(a, exact, dims=NN):
    return dot(a[0], exact, dims) + dot(a[1], exact, dims)


def pieces(x):
    a = x.astype(BF16).astype(F32)
    b = (x - a).astype(BF16).astype(F32)
    c = (x - a) - b
    return jnp.concatenate([a, b, c, jnp.zeros_like(x)], axis=0).astype(BF16)


def select(x, hot, dims=NN):
    r = dot(pieces(x), hot, dims)
    return (r[0:8] + r[8:16]) + r[16:24]


def onehot(values, count):
    ids = lax.broadcasted_iota(jnp.int32, (count, values.shape[1]), 0)
    return jnp.where(ids == values, 1.0, 0.0).astype(BF16)


def padded(x):
    return jnp.concatenate([x, jnp.zeros((M, x.shape[1]), x.dtype)], axis=0)


def padded2(x):
    return padded(x[0]), padded(x[1])


def sigmoid(x):
    return 1.0 / (1.0 + jnp.exp(-x))


def device_at(core, x, y, z):
    return (lax.rem(x, 2) * 2 + core, (z * 4 + y) * 2 + lax.div(x, 2))


def kernel(
    pos_ref, spec_ref, exp_ref, cen_ref, nbr_ref, cnt_ref, tgt_ref, rad_ref, cem_ref, nem_ref, ow_ref, env_hbm, lat_hbm,
    forces_ref, g1_ref, g2_ref,
    w_lat, w_env, latT, latN, envT, envN, a0, oc,
    tbl, ttbl, sendbuf, gsend, grecv,
    lat, xh, xl, dh, dl, sp, spp, dlat, osum, tt, pp, uu,
    h1, h2, c1, c2, ra1, ra2, rb1, rb2, rc1, rc2,
    wsem, hs, hr, ars, arr,
):
    s, b = lax.axis_index("slab"), lax.axis_index("brick")
    core, x = lax.rem(s, 2), 2 * lax.rem(b, 2) + lax.div(s, 2)
    y, z = lax.rem(lax.div(b, 2), 4), lax.div(b, 8)
    at = {"x": x, "y": y, "z": z}
    partner = device_at(1 - core, x, y, z)

    def peer(axis, k):
        c = dict(at)
        c[axis] = lax.rem(c[axis] + k, 4)
        return device_at(core, c["x"], c["y"], c["z"])

    def around(p, q):
        return (lax.rem(s + p + N_SLAB - 1, N_SLAB), lax.rem(b + q + N_BRICK - 1, N_BRICK))

    barrier = pltpu.get_barrier_semaphore()
    everyone = [around(p, q) for p, q in NEIGHBOURS] + [partner] + [peer(a, k) for a in "xyz" for k in (1, 2, 3)]
    for d in everyone:
        pl.semaphore_signal(barrier, inc=1, device_id=d, device_id_type=MESH)

    loads = [
        pltpu.make_async_copy(env_hbm, w_env, wsem.at[0]),
        pltpu.make_async_copy(lat_hbm, w_lat, wsem.at[1]),
    ]
    for c in loads:
        c.start()

    tbl[0] = jnp.zeros((8, ATOMS), F32)
    for m in range(3):
        tbl[0, m : m + 1, :] = pos_ref[m, 0]
    tbl[0, 3:4, :] = spec_ref[0].astype(F32)
    hot_exp = onehot(exp_ref[0], ATOMS)
    sendbuf[0] = select(tbl[0], hot_exp)

    pl.semaphore_wait(barrier, len(everyone))

    def halo(stage, sources, lands, back):
        out = []
        for i, (p, q) in enumerate(NEIGHBOURS):
            k = 3 * p + q
            to = around(p, q) if back else around(2 - p, 2 - q)
            out.append(
                pltpu.make_async_remote_copy(
                    src_ref=sources(k), dst_ref=lands(k), send_sem=hs.at[stage, i], recv_sem=hr.at[stage, i],
                    device_id=to, device_id_type=MESH,
                )
            )
        for c in out:
            c.start()
        return out

    sends = []
    first = halo(0, lambda k: sendbuf.at[0], lambda k: tbl.at[1 + k], False)
    sends += first

    tbl[5] = sendbuf[0]
    center = cen_ref[0]
    hot_c = onehot(center, ATOMS)
    hot_n = onehot(nbr_ref[0], 10 * ATOMS)
    same = dot(hot_c, hot_c, TN).astype(BF16)
    lane = lax.broadcasted_iota(jnp.int32, (1, E), 1)
    live = jnp.where(lane < cnt_ref[...], 1.0, 0.0)
    o_col = jnp.transpose(jnp.broadcast_to(ow_ref[...], (128, H)))
    oc[...] = jnp.concatenate([o_col, o_col], axis=1)
    a0[...] = jnp.zeros_like(a0)
    a0[0:8] = rad_ref[...]
    a0[8:13] = cem_ref[...]
    a0[16:21] = nem_ref[...]
    a0s = split(a0[...])
    for c in loads:
        c.wait()
    for l in range(2):
        w = w_lat[l]
        latN[l, 0], latN[l, 1] = split(w)
        latT[l, 0], latT[l, 1] = split(jnp.transpose(padded(w)))
        w = w_env[l]
        envT[l, 0], envT[l, 1] = split(w)
        envN[l, 0], envN[l, 1] = split(jnp.transpose(padded(w)))

    pc = select(tbl[0], hot_c)

    for c in first:
        c.wait_recv()

    row = lax.broadcasted_iota(jnp.int32, (8, 1), 0)
    blocks = [tbl[0]]
    for p in range(3):
        for q in range(3):
            t = tbl[1 + 3 * p + q]
            if (p, q) != (1, 1):
                cross_z = (lax.div(s + p - 1 + N_SLAB, N_SLAB) - 1).astype(F32) * (N_SLAB * cell_width)
                cross_y = (lax.div(b + q - 1 + N_BRICK, N_BRICK) - 1).astype(F32) * (N_BRICK * cell_width)
                t = t + jnp.where(row == 2, cross_z, 0.0) + jnp.where(row == 1, cross_y, 0.0)
            blocks.append(t)
    pn = select(jnp.concatenate(blocks, axis=1), hot_n)
    vec = jnp.where(row < 3, pn - pc, 0.0)
    squared = jnp.sum(vec * vec, axis=0, keepdims=True) + softening
    dist = jnp.sqrt(squared)
    inv_d = 1.0 / dist
    base = 1.0 - squared / (cutoff_radius * cutoff_radius)
    env = base * base * live
    direction = vec * inv_d
    order = (row + 1).astype(F32) * (math.pi / cutoff_radius)
    angle = order * dist
    sine, cosine = jnp.sin(angle), jnp.cos(angle)
    basis = sine * inv_d
    basis_d = (order * cosine - basis) * inv_d
    hot_sc = jnp.where(row.astype(F32) == pc[3:4], 1.0, 0.0)
    hot_sn = jnp.where(row.astype(F32) == pn[3:4], 1.0, 0.0)
    feats = jnp.concatenate([basis, hot_sc, hot_sn, jnp.zeros((8, E), F32)], axis=0)

    def activation(i, value):
        g = sigmoid(value)
        sp[i] = g * (1.0 + value * (1.0 - g))
        spp[i] = (g * (1.0 - g)) * (2.0 + value * (1.0 - 2.0 * g))
        return value * g

    def keep_x(l, half, rows, value):
        high, low = split(value)
        lanes = slice(E * half, E * half + E)
        xh[l, rows, lanes] = high
        xl[l, rows, lanes] = low
        return high, low

    def keep_d(l, half, value):
        high, low = split(value)
        lanes = slice(E * half, E * half + E)
        dh[l, :, lanes] = high
        dl[l, :, lanes] = low
        return high, low

    def thirds(v):
        return [v[m * M : m * M + M] for m in range(3)]

    def outer(d, w):
        return jnp.concatenate([d[m : m + 1] * w for m in range(3)], axis=0)

    def with_same(t):
        return mm2(split(t), same)

    def dotted(a, c):
        r = a * c
        return (r[0:M] + r[M : 2 * M]) + r[2 * M :]

    lat[0] = activation(0, mm3(a0s, split(feats), TN))
    for l in range(2):
        now = keep_x(l, 1, slice(0, H), lat[l])
        u = mm3((envT[l, 0], envT[l, 1]), now)
        uu[l] = u
        t = outer(direction, u * env)
        tt[l] = t
        pr = with_same(t)
        pp[l] = pr
        inv = keep_x(l, 1, slice(H, H + M), dotted(t, pr))
        update = mm3((latT[l, 0, :, 0:H], latT[l, 1, :, 0:H]), now) + mm3((latT[l, 0, :, H:], latT[l, 1, :, H:]), padded2(inv))
        lat[l + 1] = lat[l] + activation(l + 1, update)

    d_env = jnp.sum(oc[...] * lat[2], axis=0, keepdims=True)
    d_dir = [jnp.zeros((1, E), F32) for _ in range(3)]
    dlat[2] = oc[...] * env
    kept = [None, None]
    for l in (1, 0):
        delta = keep_d(l, 0, dlat[l + 1] * sp[l + 1])
        d_inv = mm3((latN[l, 0, H:], latN[l, 1, H:]), delta)
        d_inv3 = jnp.concatenate([d_inv] * 3, axis=0)
        d_t = d_inv3 * pp[l] + with_same(d_inv3 * tt[l])
        w = uu[l] * env
        d_w = dotted(outer(direction, jnp.ones((M, E), F32)), d_t)
        for m, part in enumerate(thirds(d_t)):
            d_dir[m] += jnp.sum(part * w, axis=0, keepdims=True)
        d_env += jnp.sum(d_w * uu[l], axis=0, keepdims=True)
        d_u = split(d_w * env)
        kept[l] = (d_inv3, d_t, d_w, d_u)
        back = mm3((latN[l, 0, 0:H], latN[l, 1, 0:H]), delta) + mm3((envN[l, 0], envN[l, 1]), padded2(d_u))
        dlat[l] = dlat[l + 1] + back
    delta0 = keep_d(2, 0, dlat[0] * sp[0])
    d_basis = mm3(a0s, delta0)[0:8]
    d_dir8 = jnp.concatenate(d_dir + [jnp.zeros((5, E), F32)], axis=0)
    d_dist = jnp.sum(d_basis * basis_d, axis=0, keepdims=True) - jnp.sum(d_dir8 * direction, axis=0, keepdims=True) * inv_d
    base_d = (-2.0 / (cutoff_radius * cutoff_radius)) * base * live
    d_squared = d_env * base_d + d_dist * (0.5 * inv_d)
    d_vec = d_dir8 * inv_d + 2.0 * vec * d_squared
    d_table = select(d_vec, hot_n, NT)
    own = d_table[:, 0:ATOMS] - select(d_vec, hot_c, NT)
    for k in range(9):
        gsend[k] = d_table[:, ATOMS * (k + 1) : ATOMS * (k + 2)]
    second = halo(1, lambda k: gsend.at[k], lambda k: grecv.at[k], True)
    sends += second
    for c in second:
        c.wait_recv()
    returned = gsend[4]
    for p, q in NEIGHBOURS:
        returned = returned + grecv[3 * p + q]
    total = own + select(returned, hot_exp, NT)
    ttbl[0] = jnp.zeros((8, ATOMS), F32)
    for m in range(3):
        forces_ref[m, 0] = -total[m : m + 1]
        ttbl[0, m : m + 1, :] = (2.0 / (3.0 * ATOMS)) * (total[m : m + 1] + tgt_ref[m, 0])

    sendbuf[1] = select(ttbl[0], hot_exp)
    third = halo(2, lambda k: sendbuf.at[1], lambda k: ttbl.at[1 + k], False)
    sends += third
    ttbl[5] = sendbuf[1]
    vc = select(ttbl[0], hot_c)
    for c in third:
        c.wait_recv()
    vn = select(jnp.concatenate([ttbl[k] for k in range(10)], axis=1), hot_n)
    vec_t = vn - vc
    dist_t = jnp.sum(vec * vec_t, axis=0, keepdims=True) * inv_d
    env_t = (2.0 * base_d) * (dist * dist_t)
    dir_t = (vec_t - direction * dist_t) * inv_d
    basis_t = basis_d * dist_t
    feats_t = jnp.concatenate([basis_t, jnp.zeros((24, E), F32)], axis=0)

    first_t = mm3(a0s, split(feats_t), TN)
    lat_t = sp[0] * first_t
    kept_t = [None, None]
    update_t = [None, None]
    for l in range(2):
        now = keep_x(l, 0, slice(0, H), lat_t)
        u_t = mm3((envT[l, 0], envT[l, 1]), now)
        w = uu[l] * env
        w_t = u_t * env + uu[l] * env_t
        t_t = outer(dir_t, w) + outer(direction, w_t)
        pr_t = with_same(t_t)
        inv_t = keep_x(l, 0, slice(H, H + M), dotted(t_t, pp[l]) + dotted(tt[l], pr_t))
        kept_t[l] = (t_t, pr_t)
        update_t[l] = mm3((latT[l, 0, :, 0:H], latT[l, 1, :, 0:H]), now) + mm3((latT[l, 0, :, H:], latT[l, 1, :, H:]), padded2(inv_t))
        lat_t = lat_t + sp[l + 1] * update_t[l]

    half = (h1, h2)
    from_core = (c1, c2)
    from_a, from_b, from_c = (ra1, ra2), (rb1, rb2), (rc1, rc2)
    result = (g1_ref, g2_ref)
    flying = {}

    def place(g, i):
        n = PARTS[g][i]
        row0 = sum(PARTS[g][:i])
        a, bb, c = ORDERS[i]
        row_a = row0 + at[a] * (n // 4)
        row_b = row_a + lax.div(at[bb], 2) * (n // 8)
        return n, row0, a, bb, c, pl.multiple_of(row_a, 8), pl.multiple_of(row_b, 8)

    def piece_of(row_a, n, where):
        rows = pl.ds(pl.multiple_of(row_a + lax.div(where, 2) * (n // 8), 8), n // 8)
        return rows, lax.rem(where, 2) * 128

    def copy(g, i, j, src, dst, to):
        c = pltpu.make_async_remote_copy(
            src_ref=src, dst_ref=dst, send_sem=ars.at[g, i, j], recv_sem=arr.at[g, i, j], device_id=to, device_id_type=MESH
        )
        c.start()
        sends.append(c)
        flying[g, i, j] = c

    def lands(g, i, j):
        flying[g, i, j].wait_recv()

    def lanes_at(first, count=128):
        return pl.ds(pl.multiple_of(first, 128), count)

    def start_core(g, i):
        n, row0, *_ = place(g, i)
        copy(g, i, 0, half[g].at[0, row0 : row0 + n], from_core[g].at[row0 : row0 + n], partner)

    def core_to_a(g, i):
        n, row0, a, *_ = place(g, i)
        lands(g, i, 0)
        rows = slice(row0, row0 + n)
        half[g][1, rows] = half[g][1, rows] + from_core[g][rows]
        for k in (1, 2, 3):
            theirs = row0 + lax.rem(at[a] + k, 4) * (n // 4)
            copy(g, i, k, half[g].at[1, pl.ds(pl.multiple_of(theirs, 8), n // 4)], from_a[g].at[i, k - 1], peer(a, k))

    def a_to_b(g, i):
        n, row0, a, bb, c, row_a, row_b = place(g, i)
        for k in (1, 2, 3):
            lands(g, i, k)
        rows = pl.ds(row_a, n // 4)
        half[g][1, rows] = (half[g][1, rows] + from_a[g][i, 1]) + (from_a[g][i, 0] + from_a[g][i, 2])
        for k in (1, 2, 3):
            rows, lane0 = piece_of(row_a, n, lax.rem(at[bb] + k, 4))
            copy(g, i, 3 + k, half[g].at[1, rows, lanes_at(lane0)], from_b[g].at[i, k - 1], peer(bb, k))

    def b_to_c(g, i):
        n, row0, a, bb, c, row_a, row_b = place(g, i)
        for k in (1, 2, 3):
            lands(g, i, 3 + k)
        rows, lane0 = piece_of(row_a, n, at[bb])
        lanes = lanes_at(lane0)
        half[g][1, rows, lanes] = (half[g][1, rows, lanes] + from_b[g][i, 1]) + (from_b[g][i, 0] + from_b[g][i, 2])
        for k in (1, 2, 3):
            copy(g, i, 6 + k, half[g].at[1, rows, lanes], from_c[g].at[i, k - 1], peer(c, k))

    def c_to_b(g, i):
        n, row0, a, bb, c, row_a, row_b = place(g, i)
        for k in (1, 2, 3):
            lands(g, i, 6 + k)
        rows, lane0 = piece_of(row_a, n, at[bb])
        mine = half[g][1, rows, lanes_at(lane0)]
        out = lanes_at(core * 256 + lane0)
        result[g][rows, out] = (mine + from_c[g][i, 1]) + (from_c[g][i, 0] + from_c[g][i, 2])
        for k in (1, 2, 3):
            here = result[g].at[rows, out]
            copy(g, i, 9 + k, here, here, peer(bb, k))

    def b_to_a(g, i):
        n, row0, a, bb, c, row_a, row_b = place(g, i)
        for k in (1, 2, 3):
            lands(g, i, 9 + k)
        here = result[g].at[pl.ds(row_a, n // 4), lanes_at(core * 256, 256)]
        for k in (1, 2, 3):
            copy(g, i, 12 + k, here, here, peer(a, k))

    def a_to_core(g, i):
        n, row0, *_ = place(g, i)
        for k in (1, 2, 3):
            lands(g, i, 12 + k)
        here = result[g].at[row0 : row0 + n, lanes_at(core * 256, 256)]
        copy(g, i, 16, here, here, partner)

    def finish(g, i):
        lands(g, i, 16)

    def step(g, f):
        for i in range(3):
            f(g, i)

    def gradient(l, h):
        rows = pl.ds(pl.multiple_of(h * 256, 256), 256)
        return mm3((xh[l], xl[l]), (dh[l, rows], dl[l, rows]), NT)

    lat2_t = lat_t
    scaled = oc[...] * env_t
    delta_t = keep_d(1, 1, scaled * sp[2] + dlat[2] * (spp[2] * update_t[1]))
    h1[0] = gradient(1, 1 - core)
    step(0, start_core)
    h1[1] = gradient(1, core)

    dlat_t = scaled
    env_rows = [None, None]
    for l in (1, 0):
        if l == 0:
            delta_t = keep_d(0, 1, dlat_t * sp[1] + dlat[1] * (spp[1] * update_t[0]))
            step(0, core_to_a)
        d_inv_t = mm3((latN[l, 0, H:], latN[l, 1, H:]), delta_t)
        d_inv3, d_t, d_w, d_u = kept[l]
        t_t, pr_t = kept_t[l]
        d_inv3_t = jnp.concatenate([d_inv_t] * 3, axis=0)
        d_t_t = d_inv3_t * pp[l] + d_inv3 * pr_t + with_same(d_inv3_t * tt[l] + d_inv3 * t_t)
        ones = jnp.ones((M, E), F32)
        d_w_t = dotted(outer(dir_t, ones), d_t) + dotted(outer(direction, ones), d_t_t)
        d_u_t = split(d_w_t * env + d_w * env_t)
        env_rows[l] = (jnp.concatenate([d_u[0], d_u_t[0]], axis=1), jnp.concatenate([d_u[1], d_u_t[1]], axis=1))
        back = mm3((latN[l, 0, 0:H], latN[l, 1, 0:H]), delta_t) + mm3((envN[l, 0], envN[l, 1]), padded2(d_u_t))
        dlat_t = dlat_t + back
    step(0, a_to_b)
    keep_d(2, 1, dlat_t * sp[0] + dlat[0] * (spp[0] * first_t))
    feats2 = split(jnp.concatenate([feats_t, feats], axis=1))
    out_sum = split(lat2_t * env + lat[2] * env_t)
    osum[0], osum[1] = out_sum
    ones = jnp.ones((16, E), BF16)

    def rest(h, slot):
        rows = pl.ds(pl.multiple_of(h * 256, 256), 256)
        h2[slot, 0:576] = gradient(0, h)
        for l in (1, 0):
            h2[slot, 640 - 64 * l : 704 - 64 * l] = mm3(env_rows[l], (xh[l, rows], xl[l, rows]), NT)
        h2[slot, 704:736] = mm3(feats2, (dh[2, rows], dl[2, rows]), NT)
        o = dot(ones, osum[0, rows], NT) + dot(ones, osum[1, rows], NT)
        h2[slot, 728:736] = o[0:8]
        h2[slot, 736:768] = jnp.zeros((32, 256), F32)

    rest(1 - core, 0)
    step(1, start_core)
    rest(core, 1)
    step(0, b_to_c)
    step(1, core_to_a)
    step(0, c_to_b)
    step(1, a_to_b)
    step(0, b_to_a)
    step(1, b_to_c)
    step(0, a_to_core)
    step(1, c_to_b)
    step(1, b_to_a)
    step(0, finish)
    step(1, a_to_core)
    step(1, finish)
    for c in sends:
        c.wait_send()


def unpack(g1_ref, g2_ref, rad_ref, cem_ref, nem_ref, env_ref, lat_ref, out_ref):
    lat_ref[1] = g1_ref[...]
    lat_ref[0] = g2_ref[0:576]
    env_ref[1] = g2_ref[576:640]
    env_ref[0] = g2_ref[640:704]
    rad_ref[...] = g2_ref[704:712]
    cem_ref[...] = g2_ref[712:717]
    nem_ref[...] = g2_ref[720:725]
    out_ref[...] = g2_ref[728:729]


def shape(*dims):
    return jax.ShapeDtypeStruct(dims, F32)


def on_device(
    positions, species, export_index, edge_center, edge_neighbor, edge_count, force_target, radial_weight, center_embed,
    neighbor_embed, environment_weight, latent_weight, output_weight,
):
    vmem = pl.BlockSpec(memory_space=VMEM)
    scratch = [
        VMEM((2, 576, 512), F32),
        VMEM((2, 64, 512), F32),
        VMEM((2, 2, 512, 640), BF16),
        VMEM((2, 2, 576, 512), BF16),
        VMEM((2, 2, 64, 512), BF16),
        VMEM((2, 2, 512, 128), BF16),
        VMEM((32, 512), F32),
        VMEM((H, E), F32),
        VMEM((10, 8, 128), F32),
        VMEM((10, 8, 128), F32),
        VMEM((2, 8, 128), F32),
        VMEM((9, 8, 128), F32),
        VMEM((9, 8, 128), F32),
        VMEM((3, H, E), F32),
        VMEM((2, 576, 512), BF16),
        VMEM((2, 576, 512), BF16),
        VMEM((3, 512, 512), BF16),
        VMEM((3, 512, 512), BF16),
        VMEM((3, H, E), F32),
        VMEM((3, H, E), F32),
        VMEM((3, H, E), F32),
        VMEM((2, H, E), BF16),
        VMEM((2, 3 * M, E), F32),
        VMEM((2, 3 * M, E), F32),
        VMEM((2, M, E), F32),
    ]
    for n in ROWS:
        scratch.append(VMEM((2, n, 256), F32))
    for n in ROWS:
        scratch.append(VMEM((n, 256), F32))
    for n in PARTS:
        scratch.append(VMEM((3, 3, n[0] // 4, 256), F32))
    for _ in range(2):
        for n in PARTS:
            scratch.append(VMEM((3, 3, n[0] // 8, 128), F32))
    scratch += [
        pltpu.SemaphoreType.DMA((2,)),
        pltpu.SemaphoreType.DMA((3, 8)),
        pltpu.SemaphoreType.DMA((3, 8)),
        pltpu.SemaphoreType.DMA((2, 3, 17)),
        pltpu.SemaphoreType.DMA((2, 3, 17)),
    ]
    any_space = pl.BlockSpec(memory_space=pl.ANY)
    forces, g1, g2 = pl.pallas_call(
        kernel,
        out_shape=(shape(3, 1, 1, ATOMS), shape(ROWS[0], 512), shape(ROWS[1], 512)),
        in_specs=[vmem] * 11 + [any_space] * 2,
        out_specs=(vmem,) * 3,
        scratch_shapes=scratch,
        compiler_params=pltpu.CompilerParams(collective_id=0, has_side_effects=True, vmem_limit_bytes=56 << 20),
        name="step",
    )(
        positions, species, export_index, edge_center, edge_neighbor, edge_count, force_target, radial_weight, center_embed,
        neighbor_embed, output_weight.reshape(1, 512), jnp.swapaxes(environment_weight, 1, 2), latent_weight,
    )
    grads = pl.pallas_call(
        unpack,
        out_shape=(shape(8, 512), shape(5, 512), shape(5, 512), shape(2, 64, 512), shape(2, 576, 512), shape(1, 512)),
        in_specs=[vmem] * 2,
        out_specs=(vmem,) * 6,
        compiler_params=pltpu.CompilerParams(vmem_limit_bytes=32 << 20),
        name="unpack",
    )(g1, g2)
    radial, near, far, environment, latent, output = grads
    return forces, radial, near, far, jnp.swapaxes(environment, 1, 2), latent, output.reshape(512)


def solution(mesh):
    return jax.shard_map(
        on_device,
        mesh=mesh,
        in_specs=(
            P(None, "slab", "brick", None),
            P("slab", "brick", None),
            P("slab", "brick", None),
            P("slab", "brick", None),
            P("slab", "brick", None),
            P("slab", "brick"),
            P(None, "slab", "brick", None),
            P(),
            P(),
            P(),
            P(),
            P(),
            P(),
        ),
        out_specs=(P(None, "slab", "brick", None), P(), P(), P(), P(), P(), P()),
        check_vma=False,
    )
```

```python
import math

import jax
import jax.numpy as jnp
from jax import lax
from jax.experimental import pallas as pl
from jax.experimental.pallas import tpu as pltpu
from jax.sharding import PartitionSpec as P

F32 = jnp.float32
BF16 = jnp.bfloat16
MESH = pl.DeviceIdType.MESH
VMEM = pltpu.VMEM
NN = (((1,), (0,)), ((), ()))
NT = (((1,), (1,)), ((), ()))
TN = (((0,), (0,)), ((), ()))

cell_width = 1.75
cutoff_radius = 6.0
softening = 0.25

N_SLAB, N_BRICK = 4, 32
H, M, E, ATOMS = 512, 64, 256, 128
ROWS = (576, 576, 192)
PARTS = tuple((n // 3,) * 3 for n in ROWS)
ORDERS = (("x", "y", "z"), ("y", "z", "x"), ("z", "x", "y"))
NEIGHBOURS = [(p, q) for p in range(3) for q in range(3) if (p, q) != (1, 1)]


def dot(a, b, dims=NN):
    return lax.dot_general(a, b, dims, preferred_element_type=F32)


def split(x):
    high = x.astype(BF16)
    return high, (x - high.astype(F32)).astype(BF16)


def mm3(a, b, dims=NN):
    return dot(a[0], b[0], dims) + (dot(a[0], b[1], dims) + dot(a[1], b[0], dims))


def mm2(a, exact, dims=NN):
    return dot(a[0], exact, dims) + dot(a[1], exact, dims)


def pieces(x):
    a = x.astype(BF16).astype(F32)
    b = (x - a).astype(BF16).astype(F32)
    c = (x - a) - b
    return jnp.concatenate([a, b, c, jnp.zeros_like(x)], axis=0).astype(BF16)


def select(x, hot, dims=NN):
    r = dot(pieces(x), hot, dims)
    return (r[0:8] + r[8:16]) + r[16:24]


def onehot(values, count):
    ids = lax.broadcasted_iota(jnp.int32, (count, values.shape[1]), 0)
    return jnp.where(ids == values, 1.0, 0.0).astype(BF16)


def padded(x):
    return jnp.concatenate([x, jnp.zeros((M, x.shape[1]), x.dtype)], axis=0)


def padded2(x):
    return padded(x[0]), padded(x[1])


def sigmoid(x):
    return 1.0 / (1.0 + jnp.exp(-x))


def device_at(core, x, y, z):
    return (lax.rem(x, 2) * 2 + core, (z * 4 + y) * 2 + lax.div(x, 2))


def kernel(
    pos_ref, spec_ref, exp_ref, cen_ref, nbr_ref, cnt_ref, tgt_ref, rad_ref, cem_ref, nem_ref, ow_ref, env_hbm, lat_hbm,
    forces_ref, g1_ref, g2_ref, g3_ref,
    w_lat, w_env, latT, latN, envT, envN, a0, oc,
    tbl, ttbl, sendbuf, gsend, grecv,
    lat, xh, xl, dh, dl, sp, spp, dlat, osum, tt, pp, uu,
    h1, h2, h3, c1, c2, c3, ra1, ra2, ra3, rb1, rb2, rb3, rc1, rc2, rc3,
    wsem, hs, hr, ars, arr,
):
    s, b = lax.axis_index("slab"), lax.axis_index("brick")
    core, x = lax.rem(s, 2), 2 * lax.rem(b, 2) + lax.div(s, 2)
    y, z = lax.rem(lax.div(b, 2), 4), lax.div(b, 8)
    at = {"x": x, "y": y, "z": z}
    partner = device_at(1 - core, x, y, z)

    def peer(axis, k):
        c = dict(at)
        c[axis] = lax.rem(c[axis] + k, 4)
        return device_at(core, c["x"], c["y"], c["z"])

    def around(p, q):
        return (lax.rem(s + p + N_SLAB - 1, N_SLAB), lax.rem(b + q + N_BRICK - 1, N_BRICK))

    barrier = pltpu.get_barrier_semaphore()
    everyone = [around(p, q) for p, q in NEIGHBOURS] + [partner] + [peer(a, k) for a in "xyz" for k in (1, 2, 3)]
    for d in everyone:
        pl.semaphore_signal(barrier, inc=1, device_id=d, device_id_type=MESH)

    loads = [
        pltpu.make_async_copy(env_hbm, w_env, wsem.at[0]),
        pltpu.make_async_copy(lat_hbm, w_lat, wsem.at[1]),
    ]
    for c in loads:
        c.start()

    tbl[0] = jnp.zeros((8, ATOMS), F32)
    for m in range(3):
        tbl[0, m : m + 1, :] = pos_ref[m, 0]
    tbl[0, 3:4, :] = spec_ref[0].astype(F32)
    hot_exp = onehot(exp_ref[0], ATOMS)
    sendbuf[0] = select(tbl[0], hot_exp)

    pl.semaphore_wait(barrier, len(everyone))

    def halo(stage, sources, lands, back):
        out = []
        for i, (p, q) in enumerate(NEIGHBOURS):
            k = 3 * p + q
            to = around(p, q) if back else around(2 - p, 2 - q)
            out.append(
                pltpu.make_async_remote_copy(
                    src_ref=sources(k), dst_ref=lands(k), send_sem=hs.at[stage, i], recv_sem=hr.at[stage, i],
                    device_id=to, device_id_type=MESH,
                )
            )
        for c in out:
            c.start()
        return out

    sends = []
    first = halo(0, lambda k: sendbuf.at[0], lambda k: tbl.at[1 + k], False)
    sends += first

    tbl[5] = sendbuf[0]
    center = cen_ref[0]
    hot_c = onehot(center, ATOMS)
    hot_n = onehot(nbr_ref[0], 10 * ATOMS)
    same = dot(hot_c, hot_c, TN).astype(BF16)
    lane = lax.broadcasted_iota(jnp.int32, (1, E), 1)
    live = jnp.where(lane < cnt_ref[...], 1.0, 0.0)
    o_col = jnp.transpose(jnp.broadcast_to(ow_ref[...], (128, H)))
    oc[...] = jnp.concatenate([o_col, o_col], axis=1)
    a0[...] = jnp.zeros_like(a0)
    a0[0:8] = rad_ref[...]
    a0[8:13] = cem_ref[...]
    a0[16:21] = nem_ref[...]
    a0s = split(a0[...])
    for c in loads:
        c.wait()
    for l in range(2):
        w = w_lat[l]
        latN[l, 0], latN[l, 1] = split(w)
        latT[l, 0], latT[l, 1] = split(jnp.transpose(padded(w)))
        w = w_env[l]
        envT[l, 0], envT[l, 1] = split(w)
        envN[l, 0], envN[l, 1] = split(jnp.transpose(padded(w)))

    pc = select(tbl[0], hot_c)

    for c in first:
        c.wait_recv()

    row = lax.broadcasted_iota(jnp.int32, (8, 1), 0)
    blocks = [tbl[0]]
    for p in range(3):
        for q in range(3):
            t = tbl[1 + 3 * p + q]
            if (p, q) != (1, 1):
                cross_z = (lax.div(s + p - 1 + N_SLAB, N_SLAB) - 1).astype(F32) * (N_SLAB * cell_width)
                cross_y = (lax.div(b + q - 1 + N_BRICK, N_BRICK) - 1).astype(F32) * (N_BRICK * cell_width)
                t = t + jnp.where(row == 2, cross_z, 0.0) + jnp.where(row == 1, cross_y, 0.0)
            blocks.append(t)
    pn = select(jnp.concatenate(blocks, axis=1), hot_n)
    vec = jnp.where(row < 3, pn - pc, 0.0)
    squared = jnp.sum(vec * vec, axis=0, keepdims=True) + softening
    dist = jnp.sqrt(squared)
    inv_d = 1.0 / dist
    base = 1.0 - squared / (cutoff_radius * cutoff_radius)
    env = base * base * live
    direction = vec * inv_d
    order = (row + 1).astype(F32) * (math.pi / cutoff_radius)
    angle = order * dist
    sine, cosine = jnp.sin(angle), jnp.cos(angle)
    basis = sine * inv_d
    basis_d = (order * cosine - basis) * inv_d
    hot_sc = jnp.where(row.astype(F32) == pc[3:4], 1.0, 0.0)
    hot_sn = jnp.where(row.astype(F32) == pn[3:4], 1.0, 0.0)
    feats = jnp.concatenate([basis, hot_sc, hot_sn, jnp.zeros((8, E), F32)], axis=0)

    def activation(i, value):
        g = sigmoid(value)
        sp[i] = g * (1.0 + value * (1.0 - g))
        spp[i] = value
        return value * g

    def second_derivative(i):
        value = spp[i]
        g = sigmoid(value)
        spp[i] = (g * (1.0 - g)) * (2.0 + value * (1.0 - 2.0 * g))

    def keep_x(l, half, rows, value):
        high, low = split(value)
        lanes = slice(E * half, E * half + E)
        xh[l, rows, lanes] = high
        xl[l, rows, lanes] = low
        return high, low

    def keep_d(l, half, value):
        high, low = split(value)
        lanes = slice(E * half, E * half + E)
        dh[l, :, lanes] = high
        dl[l, :, lanes] = low
        return high, low

    def thirds(v):
        return [v[m * M : m * M + M] for m in range(3)]

    def outer(d, w):
        return jnp.concatenate([d[m : m + 1] * w for m in range(3)], axis=0)

    def with_same(t):
        return mm2(split(t), same)

    def dotted(a, c):
        r = a * c
        return (r[0:M] + r[M : 2 * M]) + r[2 * M :]

    lat[0] = activation(0, mm3(a0s, split(feats), TN))
    for l in range(2):
        now = keep_x(l, 1, slice(0, H), lat[l])
        u = mm3((envT[l, 0], envT[l, 1]), now)
        uu[l] = u
        t = outer(direction, u * env)
        tt[l] = t
        pr = with_same(t)
        pp[l] = pr
        inv = keep_x(l, 1, slice(H, H + M), dotted(t, pr))
        update = mm3((latT[l, 0, :, 0:H], latT[l, 1, :, 0:H]), now) + mm3((latT[l, 0, :, H:], latT[l, 1, :, H:]), padded2(inv))
        lat[l + 1] = lat[l] + activation(l + 1, update)

    d_env = jnp.sum(oc[...] * lat[2], axis=0, keepdims=True)
    d_dir = [jnp.zeros((1, E), F32) for _ in range(3)]
    dlat[2] = oc[...] * env
    kept = [None, None]
    for l in (1, 0):
        delta = keep_d(l, 0, dlat[l + 1] * sp[l + 1])
        d_inv = mm3((latN[l, 0, H:], latN[l, 1, H:]), delta)
        d_inv3 = jnp.concatenate([d_inv] * 3, axis=0)
        d_t = d_inv3 * pp[l] + with_same(d_inv3 * tt[l])
        w = uu[l] * env
        d_w = dotted(outer(direction, jnp.ones((M, E), F32)), d_t)
        for m, part in enumerate(thirds(d_t)):
            d_dir[m] += jnp.sum(part * w, axis=0, keepdims=True)
        d_env += jnp.sum(d_w * uu[l], axis=0, keepdims=True)
        d_u = split(d_w * env)
        kept[l] = (d_inv3, d_t, d_w, d_u)
        back = mm3((latN[l, 0, 0:H], latN[l, 1, 0:H]), delta) + mm3((envN[l, 0], envN[l, 1]), padded2(d_u))
        dlat[l] = dlat[l + 1] + back
    delta0 = keep_d(2, 0, dlat[0] * sp[0])
    d_basis = mm3(a0s, delta0)[0:8]
    d_dir8 = jnp.concatenate(d_dir + [jnp.zeros((5, E), F32)], axis=0)
    d_dist = jnp.sum(d_basis * basis_d, axis=0, keepdims=True) - jnp.sum(d_dir8 * direction, axis=0, keepdims=True) * inv_d
    base_d = (-2.0 / (cutoff_radius * cutoff_radius)) * base * live
    d_squared = d_env * base_d + d_dist * (0.5 * inv_d)
    d_vec = d_dir8 * inv_d + 2.0 * vec * d_squared
    d_table = select(d_vec, hot_n, NT)
    own = d_table[:, 0:ATOMS] - select(d_vec, hot_c, NT)
    for k in range(9):
        gsend[k] = d_table[:, ATOMS * (k + 1) : ATOMS * (k + 2)]
    second = halo(1, lambda k: gsend.at[k], lambda k: grecv.at[k], True)
    sends += second
    second_derivative(0)
    second_derivative(1)
    for c in second:
        c.wait_recv()
    returned = gsend[4]
    for p, q in NEIGHBOURS:
        returned = returned + grecv[3 * p + q]
    total = own + select(returned, hot_exp, NT)
    ttbl[0] = jnp.zeros((8, ATOMS), F32)
    for m in range(3):
        forces_ref[m, 0] = -total[m : m + 1]
        ttbl[0, m : m + 1, :] = (2.0 / (3.0 * ATOMS)) * (total[m : m + 1] + tgt_ref[m, 0])

    sendbuf[1] = select(ttbl[0], hot_exp)
    third = halo(2, lambda k: sendbuf.at[1], lambda k: ttbl.at[1 + k], False)
    sends += third
    ttbl[5] = sendbuf[1]
    second_derivative(2)
    vc = select(ttbl[0], hot_c)
    for c in third:
        c.wait_recv()
    vn = select(jnp.concatenate([ttbl[k] for k in range(10)], axis=1), hot_n)
    vec_t = vn - vc
    dist_t = jnp.sum(vec * vec_t, axis=0, keepdims=True) * inv_d
    env_t = (2.0 * base_d) * (dist * dist_t)
    dir_t = (vec_t - direction * dist_t) * inv_d
    basis_t = basis_d * dist_t
    feats_t = jnp.concatenate([basis_t, jnp.zeros((24, E), F32)], axis=0)

    first_t = mm3(a0s, split(feats_t), TN)
    lat_t = sp[0] * first_t
    kept_t = [None, None]
    update_t = [None, None]
    for l in range(2):
        now = keep_x(l, 0, slice(0, H), lat_t)
        u_t = mm3((envT[l, 0], envT[l, 1]), now)
        w = uu[l] * env
        w_t = u_t * env + uu[l] * env_t
        t_t = outer(dir_t, w) + outer(direction, w_t)
        pr_t = with_same(t_t)
        inv_t = keep_x(l, 0, slice(H, H + M), dotted(t_t, pp[l]) + dotted(tt[l], pr_t))
        kept_t[l] = (t_t, pr_t)
        update_t[l] = mm3((latT[l, 0, :, 0:H], latT[l, 1, :, 0:H]), now) + mm3((latT[l, 0, :, H:], latT[l, 1, :, H:]), padded2(inv_t))
        lat_t = lat_t + sp[l + 1] * update_t[l]

    half = (h1, h2, h3)
    from_core = (c1, c2, c3)
    from_a, from_b, from_c = (ra1, ra2, ra3), (rb1, rb2, rb3), (rc1, rc2, rc3)
    result = (g1_ref, g2_ref, g3_ref)
    flying = {}

    def place(g, i):
        n = PARTS[g][i]
        row0 = sum(PARTS[g][:i])
        a, bb, c = ORDERS[i]
        row_a = row0 + at[a] * (n // 4)
        row_b = row_a + lax.div(at[bb], 2) * (n // 8)
        return n, row0, a, bb, c, pl.multiple_of(row_a, 8), pl.multiple_of(row_b, 8)

    def piece_of(row_a, n, where):
        rows = pl.ds(pl.multiple_of(row_a + lax.div(where, 2) * (n // 8), 8), n // 8)
        return rows, lax.rem(where, 2) * 128

    def copy(g, i, j, src, dst, to):
        c = pltpu.make_async_remote_copy(
            src_ref=src, dst_ref=dst, send_sem=ars.at[g, i, j], recv_sem=arr.at[g, i, j], device_id=to, device_id_type=MESH
        )
        c.start()
        sends.append(c)
        flying[g, i, j] = c

    def lands(g, i, j):
        flying[g, i, j].wait_recv()

    def lanes_at(first, count=128):
        return pl.ds(pl.multiple_of(first, 128), count)

    def chunk(g, i, k):
        n, row0, a, *_ = place(g, i)
        return pl.ds(pl.multiple_of(row0 + lax.rem(at[a] + k, 4) * (n // 4), 8), n // 4)

    def start_core(g):
        for k in (2, 1, 3, 0):
            for i in range(3):
                rows = chunk(g, i, k)
                copy(g, i, 16 + k, half[g].at[0, rows], from_core[g].at[rows], partner)

    def core_to_a(g):
        for k in (2, 1, 3, 0):
            for i in range(3):
                lands(g, i, 16 + k)
                rows = chunk(g, i, k)
                half[g][1, rows] = half[g][1, rows] + from_core[g][rows]
                if k:
                    a = ORDERS[i][0]
                    copy(g, i, k, half[g].at[1, rows], from_a[g].at[i, k - 1], peer(a, k))

    def a_to_b(g, i):
        n, row0, a, bb, c, row_a, row_b = place(g, i)
        for k in (1, 2, 3):
            lands(g, i, k)
        rows = pl.ds(row_a, n // 4)
        half[g][1, rows] = (half[g][1, rows] + from_a[g][i, 1]) + (from_a[g][i, 0] + from_a[g][i, 2])
        for k in (1, 2, 3):
            rows, lane0 = piece_of(row_a, n, lax.rem(at[bb] + k, 4))
            copy(g, i, 3 + k, half[g].at[1, rows, lanes_at(lane0)], from_b[g].at[i, k - 1], peer(bb, k))

    def b_to_c(g, i):
        n, row0, a, bb, c, row_a, row_b = place(g, i)
        for k in (1, 2, 3):
            lands(g, i, 3 + k)
        rows, lane0 = piece_of(row_a, n, at[bb])
        lanes = lanes_at(lane0)
        half[g][1, rows, lanes] = (half[g][1, rows, lanes] + from_b[g][i, 1]) + (from_b[g][i, 0] + from_b[g][i, 2])
        for k in (1, 2, 3):
            copy(g, i, 6 + k, half[g].at[1, rows, lanes], from_c[g].at[i, k - 1], peer(c, k))

    def c_to_b(g, i):
        n, row0, a, bb, c, row_a, row_b = place(g, i)
        for k in (1, 2, 3):
            lands(g, i, 6 + k)
        rows, lane0 = piece_of(row_a, n, at[bb])
        mine = half[g][1, rows, lanes_at(lane0)]
        out = lanes_at(core * 256 + lane0)
        result[g][rows, out] = (mine + from_c[g][i, 1]) + (from_c[g][i, 0] + from_c[g][i, 2])
        for k in (1, 2, 3):
            here = result[g].at[rows, out]
            copy(g, i, 9 + k, here, here, peer(bb, k))

    def b_to_a(g, i):
        n, row0, a, bb, c, row_a, row_b = place(g, i)
        for k in (1, 2, 3):
            lands(g, i, 9 + k)
        here = result[g].at[pl.ds(row_a, n // 4), lanes_at(core * 256, 256)]
        for k in (2, 1, 3):
            copy(g, i, 12 + k, here, here, peer(a, k))
        copy(g, i, 20, here, here, partner)

    def a_to_core(g):
        for k in (1, 3, 2):
            for i in range(3):
                lands(g, i, 12 + k)
                here = result[g].at[chunk(g, i, 4 - k), lanes_at(core * 256, 256)]
                copy(g, i, 20 + k, here, here, partner)

    def finish(g):
        for i in range(3):
            for k in range(4):
                lands(g, i, 20 + k)

    def step(g, f):
        for i in range(3):
            f(g, i)

    def gradient(l, h):
        rows = pl.ds(pl.multiple_of(h * 256, 256), 256)
        return mm3((xh[l], xl[l]), (dh[l, rows], dl[l, rows]), NT)

    lat2_t = lat_t
    scaled = oc[...] * env_t
    delta_t = keep_d(1, 1, scaled * sp[2] + dlat[2] * (spp[2] * update_t[1]))
    h1[0] = gradient(1, 1 - core)
    start_core(0)
    h1[1] = gradient(1, core)

    dlat_t = scaled
    env_rows = [None, None]
    for l in (1, 0):
        if l == 0:
            delta_t = keep_d(0, 1, dlat_t * sp[1] + dlat[1] * (spp[1] * update_t[0]))
            core_to_a(0)
            h2[0] = gradient(0, 1 - core)
            start_core(1)
            h2[1] = gradient(0, core)
        d_inv_t = mm3((latN[l, 0, H:], latN[l, 1, H:]), delta_t)
        d_inv3, d_t, d_w, d_u = kept[l]
        t_t, pr_t = kept_t[l]
        d_inv3_t = jnp.concatenate([d_inv_t] * 3, axis=0)
        d_t_t = d_inv3_t * pp[l] + d_inv3 * pr_t + with_same(d_inv3_t * tt[l] + d_inv3 * t_t)
        ones = jnp.ones((M, E), F32)
        d_w_t = dotted(outer(dir_t, ones), d_t) + dotted(outer(direction, ones), d_t_t)
        d_u_t = split(d_w_t * env + d_w * env_t)
        env_rows[l] = (jnp.concatenate([d_u[0], d_u_t[0]], axis=1), jnp.concatenate([d_u[1], d_u_t[1]], axis=1))
        back = mm3((latN[l, 0, 0:H], latN[l, 1, 0:H]), delta_t) + mm3((envN[l, 0], envN[l, 1]), padded2(d_u_t))
        dlat_t = dlat_t + back
    core_to_a(1)
    keep_d(2, 1, dlat_t * sp[0] + dlat[0] * (spp[0] * first_t))
    feats2 = split(jnp.concatenate([feats_t, feats], axis=1))
    out_sum = split(lat2_t * env + lat[2] * env_t)
    osum[0], osum[1] = out_sum
    ones = jnp.ones((16, E), BF16)

    def rest(h, slot):
        rows = pl.ds(pl.multiple_of(h * 256, 256), 256)
        for l in (1, 0):
            h3[slot, 64 - 64 * l : 128 - 64 * l] = mm3(env_rows[l], (xh[l, rows], xl[l, rows]), NT)
        h3[slot, 128:160] = mm3(feats2, (dh[2, rows], dl[2, rows]), NT)
        o = dot(ones, osum[0, rows], NT) + dot(ones, osum[1, rows], NT)
        h3[slot, 152:160] = o[0:8]
        h3[slot, 160:192] = jnp.zeros((32, 256), F32)

    rest(1 - core, 0)
    start_core(2)
    rest(core, 1)
    step(0, a_to_b)
    core_to_a(2)
    step(0, b_to_c)
    step(1, a_to_b)
    step(2, a_to_b)
    step(0, c_to_b)
    step(1, b_to_c)
    step(2, b_to_c)
    step(0, b_to_a)
    step(1, c_to_b)
    step(2, c_to_b)
    step(1, b_to_a)
    a_to_core(0)
    step(2, b_to_a)
    a_to_core(1)
    a_to_core(2)
    for g in range(3):
        finish(g)
    for c in sends:
        c.wait_send()


def unpack(f_ref, g1_ref, g2_ref, g3_ref, forces_ref, rad_ref, cem_ref, nem_ref, env_ref, lat_ref, out_ref):
    lat_ref[1] = g1_ref[...]
    lat_ref[0] = g2_ref[...]
    env_ref[1] = g3_ref[0:64]
    env_ref[0] = g3_ref[64:128]
    rad_ref[...] = g3_ref[128:136]
    cem_ref[...] = g3_ref[136:141]
    nem_ref[...] = g3_ref[144:149]
    out_ref[...] = g3_ref[152:153]
    forces_ref[...] = f_ref[...]


def shape(*dims):
    return jax.ShapeDtypeStruct(dims, F32)


def on_device(
    positions, species, export_index, edge_center, edge_neighbor, edge_count, force_target, radial_weight, center_embed,
    neighbor_embed, environment_weight, latent_weight, output_weight,
):
    vmem = pl.BlockSpec(memory_space=VMEM)
    scratch = [
        VMEM((2, 576, 512), F32),
        VMEM((2, 64, 512), F32),
        VMEM((2, 2, 512, 640), BF16),
        VMEM((2, 2, 576, 512), BF16),
        VMEM((2, 2, 64, 512), BF16),
        VMEM((2, 2, 512, 128), BF16),
        VMEM((32, 512), F32),
        VMEM((H, E), F32),
        VMEM((10, 8, 128), F32),
        VMEM((10, 8, 128), F32),
        VMEM((2, 8, 128), F32),
        VMEM((9, 8, 128), F32),
        VMEM((9, 8, 128), F32),
        VMEM((3, H, E), F32),
        VMEM((2, 576, 512), BF16),
        VMEM((2, 576, 512), BF16),
        VMEM((3, 512, 512), BF16),
        VMEM((3, 512, 512), BF16),
        VMEM((3, H, E), F32),
        VMEM((3, H, E), F32),
        VMEM((3, H, E), F32),
        VMEM((2, H, E), BF16),
        VMEM((2, 3 * M, E), F32),
        VMEM((2, 3 * M, E), F32),
        VMEM((2, M, E), F32),
    ]
    for n in ROWS:
        scratch.append(VMEM((2, n, 256), F32))
    for n in ROWS:
        scratch.append(VMEM((n, 256), F32))
    for n in PARTS:
        scratch.append(VMEM((3, 3, n[0] // 4, 256), F32))
    for _ in (1, 2):
        for n in PARTS:
            scratch.append(VMEM((3, 3, n[0] // 8, 128), F32))
    scratch += [
        pltpu.SemaphoreType.DMA((2,)),
        pltpu.SemaphoreType.DMA((3, 8)),
        pltpu.SemaphoreType.DMA((3, 8)),
        pltpu.SemaphoreType.DMA((3, 3, 24)),
        pltpu.SemaphoreType.DMA((3, 3, 24)),
    ]
    any_space = pl.BlockSpec(memory_space=pl.ANY)
    parts = pl.pallas_call(
        kernel,
        out_shape=(VMEM((3, 1, 1, ATOMS), F32),) + tuple(VMEM((n, 512), F32) for n in ROWS),
        in_specs=[vmem] * 11 + [any_space] * 2,
        out_specs=(vmem,) * 4,
        scratch_shapes=scratch,
        compiler_params=pltpu.CompilerParams(collective_id=0, has_side_effects=True, vmem_limit_bytes=56 << 20),
        name="step",
    )(
        positions, species, export_index, edge_center, edge_neighbor, edge_count, force_target, radial_weight, center_embed,
        neighbor_embed, output_weight.reshape(1, 512), jnp.swapaxes(environment_weight, 1, 2), latent_weight,
    )
    outs = pl.pallas_call(
        unpack,
        out_shape=(shape(3, 1, 1, ATOMS), shape(8, 512), shape(5, 512), shape(5, 512), shape(2, 64, 512), shape(2, 576, 512), shape(1, 512)),
        in_specs=[vmem] * 4,
        out_specs=(vmem,) * 7,
        compiler_params=pltpu.CompilerParams(vmem_limit_bytes=32 << 20),
        name="unpack",
    )(*parts)
    forces, radial, near, far, environment, latent, output = outs
    return forces, radial, near, far, jnp.swapaxes(environment, 1, 2), latent, output.reshape(512)


def solution(mesh):
    return jax.shard_map(
        on_device,
        mesh=mesh,
        in_specs=(
            P(None, "slab", "brick", None),
            P("slab", "brick", None),
            P("slab", "brick", None),
            P("slab", "brick", None),
            P("slab", "brick", None),
            P("slab", "brick"),
            P(None, "slab", "brick", None),
            P(),
            P(),
            P(),
            P(),
            P(),
            P(),
        ),
        out_specs=(P(None, "slab", "brick", None), P(), P(), P(), P(), P(), P()),
        check_vma=False,
    )
```

```python
import math

import jax
import jax.numpy as jnp
from jax import lax
from jax.experimental import pallas as pl
from jax.experimental.pallas import tpu as pltpu
from jax.sharding import PartitionSpec as P

F32 = jnp.float32
BF16 = jnp.bfloat16
MESH = pl.DeviceIdType.MESH
VMEM = pltpu.VMEM
NN = (((1,), (0,)), ((), ()))
NT = (((1,), (1,)), ((), ()))
TN = (((0,), (0,)), ((), ()))

cell_width = 1.75
cutoff_radius = 6.0
softening = 0.25

N_SLAB, N_BRICK = 4, 32
H, M, E, ATOMS = 512, 64, 256, 128
ROWS = (576, 576, 192)
PARTS = tuple((n // 3,) * 3 for n in ROWS)
ORDERS = (("x", "y", "z"), ("y", "z", "x"), ("z", "x", "y"))
NEIGHBOURS = [(p, q) for q in (0, 2, 1) for p in (0, 2, 1) if (p, q) != (1, 1)]


def dot(a, b, dims=NN):
    return lax.dot_general(a, b, dims, preferred_element_type=F32)


def split(x):
    high = x.astype(BF16)
    return high, (x - high.astype(F32)).astype(BF16)


def mm3(a, b, dims=NN):
    return dot(a[0], b[0], dims) + (dot(a[0], b[1], dims) + dot(a[1], b[0], dims))


def mm2(a, exact, dims=NN):
    return dot(a[0], exact, dims) + dot(a[1], exact, dims)


def pieces(x):
    a = x.astype(BF16).astype(F32)
    b = (x - a).astype(BF16).astype(F32)
    c = (x - a) - b
    return jnp.concatenate([a, b, c, jnp.zeros_like(x)], axis=0).astype(BF16)


def select(x, hot, dims=NN):
    r = dot(pieces(x), hot, dims)
    return (r[0:8] + r[8:16]) + r[16:24]


def onehot(values, count):
    ids = lax.broadcasted_iota(jnp.int32, (count, values.shape[1]), 0)
    return jnp.where(ids == values, 1.0, 0.0).astype(BF16)


def padded(x):
    return jnp.concatenate([x, jnp.zeros((M, x.shape[1]), x.dtype)], axis=0)


def padded2(x):
    return padded(x[0]), padded(x[1])


def sigmoid(x):
    return 1.0 / (1.0 + jnp.exp(-x))


def device_at(core, x, y, z):
    return (lax.rem(x, 2) * 2 + core, (z * 4 + y) * 2 + lax.div(x, 2))


def kernel(
    pos_ref, spec_ref, exp_ref, cen_ref, nbr_ref, cnt_ref, tgt_ref, rad_ref, cem_ref, nem_ref, ow_ref, env_hbm, lat_hbm,
    forces_ref, g1_ref, g2_ref, g3_ref,
    w_lat, w_env, latT, latN, envT, envN, a0, oc,
    tbl, ttbl, sendbuf, gsend, grecv,
    lat, xh, xl, dh, dl, sp, spp, dlat, osum, tt, pp, uu,
    h1, h2, h3, c1, c2, c3, ra1, ra2, ra3, rb1, rb2, rb3, rc1, rc2, rc3,
    wsem, hs, hr, ars, arr,
):
    s, b = lax.axis_index("slab"), lax.axis_index("brick")
    core, x = lax.rem(s, 2), 2 * lax.rem(b, 2) + lax.div(s, 2)
    y, z = lax.rem(lax.div(b, 2), 4), lax.div(b, 8)
    at = {"x": x, "y": y, "z": z}
    partner = device_at(1 - core, x, y, z)

    def peer(axis, k):
        c = dict(at)
        c[axis] = lax.rem(c[axis] + k, 4)
        return device_at(core, c["x"], c["y"], c["z"])

    def around(p, q):
        return (lax.rem(s + p + N_SLAB - 1, N_SLAB), lax.rem(b + q + N_BRICK - 1, N_BRICK))

    barrier = pltpu.get_barrier_semaphore()
    everyone = [around(p, q) for p, q in NEIGHBOURS] + [partner] + [peer(a, k) for a in "xyz" for k in (1, 2, 3)]
    for d in everyone:
        pl.semaphore_signal(barrier, inc=1, device_id=d, device_id_type=MESH)

    loads = [
        pltpu.make_async_copy(env_hbm, w_env, wsem.at[0]),
        pltpu.make_async_copy(lat_hbm, w_lat, wsem.at[1]),
    ]
    for c in loads:
        c.start()

    tbl[0] = jnp.zeros((8, ATOMS), F32)
    for m in range(3):
        tbl[0, m : m + 1, :] = pos_ref[m, 0]
    tbl[0, 3:4, :] = spec_ref[0].astype(F32)
    hot_exp = onehot(exp_ref[0], ATOMS)
    sendbuf[0] = select(tbl[0], hot_exp)

    pl.semaphore_wait(barrier, len(everyone))

    def halo(stage, sources, lands, back):
        out = []
        for i, (p, q) in enumerate(NEIGHBOURS):
            k = 3 * p + q
            to = around(p, q) if back else around(2 - p, 2 - q)
            out.append(
                pltpu.make_async_remote_copy(
                    src_ref=sources(k), dst_ref=lands(k), send_sem=hs.at[stage, i], recv_sem=hr.at[stage, i],
                    device_id=to, device_id_type=MESH,
                )
            )
        for c in out:
            c.start()
        return out

    sends = []
    first = halo(0, lambda k: sendbuf.at[0], lambda k: tbl.at[1 + k], False)
    sends += first

    tbl[5] = sendbuf[0]
    center = cen_ref[0]
    hot_c = onehot(center, ATOMS)
    hot_n = onehot(nbr_ref[0], 10 * ATOMS)
    same = dot(hot_c, hot_c, TN).astype(BF16)
    lane = lax.broadcasted_iota(jnp.int32, (1, E), 1)
    live = jnp.where(lane < cnt_ref[...], 1.0, 0.0)
    o_col = jnp.transpose(jnp.broadcast_to(ow_ref[...], (128, H)))
    oc[...] = jnp.concatenate([o_col, o_col], axis=1)
    a0[...] = jnp.zeros_like(a0)
    a0[0:8] = rad_ref[...]
    a0[8:13] = cem_ref[...]
    a0[16:21] = nem_ref[...]
    a0s = split(a0[...])
    for c in loads:
        c.wait()
    for l in range(2):
        w = w_lat[l]
        latN[l, 0], latN[l, 1] = split(w)
        latT[l, 0], latT[l, 1] = split(jnp.transpose(padded(w)))
        w = w_env[l]
        envT[l, 0], envT[l, 1] = split(w)
        envN[l, 0], envN[l, 1] = split(jnp.transpose(padded(w)))

    pc = select(tbl[0], hot_c)

    for c in first:
        c.wait_recv()

    row = lax.broadcasted_iota(jnp.int32, (8, 1), 0)
    blocks = [tbl[0]]
    for p in range(3):
        for q in range(3):
            t = tbl[1 + 3 * p + q]
            if (p, q) != (1, 1):
                cross_z = (lax.div(s + p - 1 + N_SLAB, N_SLAB) - 1).astype(F32) * (N_SLAB * cell_width)
                cross_y = (lax.div(b + q - 1 + N_BRICK, N_BRICK) - 1).astype(F32) * (N_BRICK * cell_width)
                t = t + jnp.where(row == 2, cross_z, 0.0) + jnp.where(row == 1, cross_y, 0.0)
            blocks.append(t)
    pn = select(jnp.concatenate(blocks, axis=1), hot_n)
    vec = jnp.where(row < 3, pn - pc, 0.0)
    squared = jnp.sum(vec * vec, axis=0, keepdims=True) + softening
    dist = jnp.sqrt(squared)
    inv_d = 1.0 / dist
    base = 1.0 - squared / (cutoff_radius * cutoff_radius)
    env = base * base * live
    direction = vec * inv_d
    order = (row + 1).astype(F32) * (math.pi / cutoff_radius)
    angle = order * dist
    sine, cosine = jnp.sin(angle), jnp.cos(angle)
    basis = sine * inv_d
    basis_d = (order * cosine - basis) * inv_d
    hot_sc = jnp.where(row.astype(F32) == pc[3:4], 1.0, 0.0)
    hot_sn = jnp.where(row.astype(F32) == pn[3:4], 1.0, 0.0)
    feats = jnp.concatenate([basis, hot_sc, hot_sn, jnp.zeros((8, E), F32)], axis=0)

    def activation(i, value):
        g = sigmoid(value)
        sp[i] = g * (1.0 + value * (1.0 - g))
        spp[i] = value
        return value * g

    def second_derivative(i):
        value = spp[i]
        g = sigmoid(value)
        spp[i] = (g * (1.0 - g)) * (2.0 + value * (1.0 - 2.0 * g))

    def keep_x(l, half, rows, value):
        high, low = split(value)
        lanes = slice(E * half, E * half + E)
        xh[l, rows, lanes] = high
        xl[l, rows, lanes] = low
        return high, low

    def keep_d(l, half, value):
        high, low = split(value)
        lanes = slice(E * half, E * half + E)
        dh[l, :, lanes] = high
        dl[l, :, lanes] = low
        return high, low

    def thirds(v):
        return [v[m * M : m * M + M] for m in range(3)]

    def outer(d, w):
        return jnp.concatenate([d[m : m + 1] * w for m in range(3)], axis=0)

    def with_same(t):
        return mm2(split(t), same)

    def dotted(a, c):
        r = a * c
        return (r[0:M] + r[M : 2 * M]) + r[2 * M :]

    lat[0] = activation(0, mm3(a0s, split(feats), TN))
    for l in range(2):
        now = keep_x(l, 1, slice(0, H), lat[l])
        u = mm3((envT[l, 0], envT[l, 1]), now)
        uu[l] = u
        t = outer(direction, u * env)
        tt[l] = t
        pr = with_same(t)
        pp[l] = pr
        inv = keep_x(l, 1, slice(H, H + M), dotted(t, pr))
        update = mm3((latT[l, 0, :, 0:H], latT[l, 1, :, 0:H]), now) + mm3((latT[l, 0, :, H:], latT[l, 1, :, H:]), padded2(inv))
        lat[l + 1] = lat[l] + activation(l + 1, update)

    d_env = jnp.sum(oc[...] * lat[2], axis=0, keepdims=True)
    d_dir = [jnp.zeros((1, E), F32) for _ in range(3)]
    dlat[2] = oc[...] * env
    kept = [None, None]
    for l in (1, 0):
        delta = keep_d(l, 0, dlat[l + 1] * sp[l + 1])
        d_inv = mm3((latN[l, 0, H:], latN[l, 1, H:]), delta)
        d_inv3 = jnp.concatenate([d_inv] * 3, axis=0)
        d_t = d_inv3 * pp[l] + with_same(d_inv3 * tt[l])
        w = uu[l] * env
        d_w = dotted(outer(direction, jnp.ones((M, E), F32)), d_t)
        for m, part in enumerate(thirds(d_t)):
            d_dir[m] += jnp.sum(part * w, axis=0, keepdims=True)
        d_env += jnp.sum(d_w * uu[l], axis=0, keepdims=True)
        d_u = split(d_w * env)
        kept[l] = (d_inv3, d_t, d_w, d_u)
        back = mm3((latN[l, 0, 0:H], latN[l, 1, 0:H]), delta) + mm3((envN[l, 0], envN[l, 1]), padded2(d_u))
        dlat[l] = dlat[l + 1] + back
    delta0 = keep_d(2, 0, dlat[0] * sp[0])
    d_basis = mm3(a0s, delta0)[0:8]
    d_dir8 = jnp.concatenate(d_dir + [jnp.zeros((5, E), F32)], axis=0)
    d_dist = jnp.sum(d_basis * basis_d, axis=0, keepdims=True) - jnp.sum(d_dir8 * direction, axis=0, keepdims=True) * inv_d
    base_d = (-2.0 / (cutoff_radius * cutoff_radius)) * base * live
    d_squared = d_env * base_d + d_dist * (0.5 * inv_d)
    d_vec = d_dir8 * inv_d + 2.0 * vec * d_squared
    d_table = select(d_vec, hot_n, NT)
    own = d_table[:, 0:ATOMS] - select(d_vec, hot_c, NT)
    for k in range(9):
        gsend[k] = d_table[:, ATOMS * (k + 1) : ATOMS * (k + 2)]
    second = halo(1, lambda k: gsend.at[k], lambda k: grecv.at[k], True)
    sends += second
    second_derivative(0)
    second_derivative(1)
    for c in second:
        c.wait_recv()
    returned = gsend[4]
    for p, q in NEIGHBOURS:
        returned = returned + grecv[3 * p + q]
    total = own + select(returned, hot_exp, NT)
    ttbl[0] = jnp.zeros((8, ATOMS), F32)
    for m in range(3):
        forces_ref[m, 0] = -total[m : m + 1]
        ttbl[0, m : m + 1, :] = (2.0 / (3.0 * ATOMS)) * (total[m : m + 1] + tgt_ref[m, 0])

    sendbuf[1] = select(ttbl[0], hot_exp)
    third = halo(2, lambda k: sendbuf.at[1], lambda k: ttbl.at[1 + k], False)
    sends += third
    ttbl[5] = sendbuf[1]
    second_derivative(2)
    vc = select(ttbl[0], hot_c)
    for c in third:
        c.wait_recv()
    vn = select(jnp.concatenate([ttbl[k] for k in range(10)], axis=1), hot_n)
    vec_t = vn - vc
    dist_t = jnp.sum(vec * vec_t, axis=0, keepdims=True) * inv_d
    env_t = (2.0 * base_d) * (dist * dist_t)
    dir_t = (vec_t - direction * dist_t) * inv_d
    basis_t = basis_d * dist_t
    feats_t = jnp.concatenate([basis_t, jnp.zeros((24, E), F32)], axis=0)

    first_t = mm3(a0s, split(feats_t), TN)
    lat_t = sp[0] * first_t
    kept_t = [None, None]
    update_t = [None, None]
    for l in range(2):
        now = keep_x(l, 0, slice(0, H), lat_t)
        u_t = mm3((envT[l, 0], envT[l, 1]), now)
        w = uu[l] * env
        w_t = u_t * env + uu[l] * env_t
        t_t = outer(dir_t, w) + outer(direction, w_t)
        pr_t = with_same(t_t)
        inv_t = keep_x(l, 0, slice(H, H + M), dotted(t_t, pp[l]) + dotted(tt[l], pr_t))
        kept_t[l] = (t_t, pr_t)
        update_t[l] = mm3((latT[l, 0, :, 0:H], latT[l, 1, :, 0:H]), now) + mm3((latT[l, 0, :, H:], latT[l, 1, :, H:]), padded2(inv_t))
        lat_t = lat_t + sp[l + 1] * update_t[l]

    half = (h1, h2, h3)
    from_core = (c1, c2, c3)
    from_a, from_b, from_c = (ra1, ra2, ra3), (rb1, rb2, rb3), (rc1, rc2, rc3)
    result = (g1_ref, g2_ref, g3_ref)
    flying, done = {}, []

    def place(g, i):
        n = PARTS[g][i]
        row0 = sum(PARTS[g][:i])
        a, bb, c = ORDERS[i]
        row_a = row0 + at[a] * (n // 4)
        row_b = row_a + lax.div(at[bb], 2) * (n // 8)
        return n, row0, a, bb, c, pl.multiple_of(row_a, 8), pl.multiple_of(row_b, 8)

    def piece_of(row_a, n, where):
        rows = pl.ds(pl.multiple_of(row_a + lax.div(where, 2) * (n // 8), 8), n // 8)
        return rows, lax.rem(where, 2) * 128

    def copy(g, i, j, src, dst, to):
        c = pltpu.make_async_remote_copy(
            src_ref=src, dst_ref=dst, send_sem=ars.at[g, i, j], recv_sem=arr.at[g, i, j], device_id=to, device_id_type=MESH
        )
        c.start()
        sends.append(c)
        flying[g, i, j] = c

    def lands(g, i, j):
        flying[g, i, j].wait_recv()

    def lanes_at(first, count=128):
        return pl.ds(pl.multiple_of(first, 128), count)

    def chunk(g, i, k):
        n, row0, a, *_ = place(g, i)
        return pl.ds(pl.multiple_of(row0 + lax.rem(at[a] + k, 4) * (n // 4), 8), n // 4)

    def start_core(g):
        for k in (2, 1, 3, 0):
            for i in range(3):
                rows = chunk(g, i, k)
                copy(g, i, 16 + k, half[g].at[0, rows], from_core[g].at[rows], partner)

    def core_to_a(g):
        for k in (2, 1, 3, 0):
            for i in range(3):
                lands(g, i, 16 + k)
                rows = chunk(g, i, k)
                half[g][1, rows] = half[g][1, rows] + from_core[g][rows]
                if k:
                    a = ORDERS[i][0]
                    copy(g, i, k, half[g].at[1, rows], from_a[g].at[i, k - 1], peer(a, k))

    def a_to_b(g, i):
        n, row0, a, bb, c, row_a, row_b = place(g, i)
        for k in (1, 2, 3):
            lands(g, i, k)
        rows = pl.ds(row_a, n // 4)
        half[g][1, rows] = (half[g][1, rows] + from_a[g][i, 1]) + (from_a[g][i, 0] + from_a[g][i, 2])
        for k in (1, 2, 3):
            rows, lane0 = piece_of(row_a, n, lax.rem(at[bb] + k, 4))
            copy(g, i, 3 + k, half[g].at[1, rows, lanes_at(lane0)], from_b[g].at[i, k - 1], peer(bb, k))

    def b_to_c(g, i):
        n, row0, a, bb, c, row_a, row_b = place(g, i)
        for k in (1, 2, 3):
            lands(g, i, 3 + k)
        rows, lane0 = piece_of(row_a, n, at[bb])
        lanes = lanes_at(lane0)
        half[g][1, rows, lanes] = (half[g][1, rows, lanes] + from_b[g][i, 1]) + (from_b[g][i, 0] + from_b[g][i, 2])
        for k in (1, 2, 3):
            copy(g, i, 6 + k, half[g].at[1, rows, lanes], from_c[g].at[i, k - 1], peer(c, k))

    def c_to_b(g, i):
        n, row0, a, bb, c, row_a, row_b = place(g, i)
        for k in (1, 2, 3):
            lands(g, i, 6 + k)
        rows, lane0 = piece_of(row_a, n, at[bb])
        mine = half[g][1, rows, lanes_at(lane0)]
        out = lanes_at(core * 256 + lane0)
        result[g][rows, out] = (mine + from_c[g][i, 1]) + (from_c[g][i, 0] + from_c[g][i, 2])
        for k in (1, 2, 3):
            here = result[g].at[rows, out]
            copy(g, i, 9 + k, here, here, peer(bb, k))

    def b_to_a(g, i):
        n, row0, a, bb, c, row_a, row_b = place(g, i)
        for k in (1, 2, 3):
            lands(g, i, 9 + k)
        here = result[g].at[pl.ds(row_a, n // 4), lanes_at(core * 256, 256)]
        for k in (2, 1, 3):
            copy(g, i, 12 + k, here, here, peer(a, k))
        copy(g, i, 20, here, here, partner)

    def a_to_core(g):
        for k in (1, 3, 2):
            for i in range(3):
                lands(g, i, 12 + k)
                here = result[g].at[chunk(g, i, 4 - k), lanes_at(core * 256, 256)]
                copy(g, i, 20 + k, here, here, partner)

    def finish(g):
        for i in range(3):
            for k in range(4):
                lands(g, i, 20 + k)

    def whole_chunk(g, i):
        row_a = place(g, i)[5]
        return half[g].at[1, pl.ds(row_a, PARTS[g][i] // 4)]

    def exchange(g, i, first, came_from, axis):
        here = whole_chunk(g, i)
        for k in (2, 1, 3):
            copy(g, i, first + k, here, came_from[g].at[i, k - 1], peer(axis, k))

    def a_to_b_whole(g, i):
        for k in (1, 2, 3):
            lands(g, i, k)
        here = whole_chunk(g, i)
        here[...] = (here[...] + from_a[g][i, 1]) + (from_a[g][i, 0] + from_a[g][i, 2])
        exchange(g, i, 3, from_b, ORDERS[i][1])

    def b_to_c_whole(g, i):
        for k in (1, 2, 3):
            lands(g, i, 3 + k)
            flying[g, i, 3 + k].wait_send()
            done.append(flying[g, i, 3 + k])
        here = whole_chunk(g, i)
        here[...] = (here[...] + from_b[g][i, 1]) + (from_b[g][i, 0] + from_b[g][i, 2])
        exchange(g, i, 6, from_c, ORDERS[i][2])

    def c_to_a_whole(g, i):
        for k in (1, 2, 3):
            lands(g, i, 6 + k)
        n, row0, a, bb, c, row_a, row_b = place(g, i)
        out = result[g].at[pl.ds(row_a, n // 4), lanes_at(core * 256, 256)]
        here = whole_chunk(g, i)
        out[...] = (here[...] + from_c[g][i, 1]) + (from_c[g][i, 0] + from_c[g][i, 2])
        for k in (2, 1, 3):
            copy(g, i, 12 + k, out, out, peer(a, k))
        copy(g, i, 20, out, out, partner)

    def step(g, f):
        for i in range(3):
            f(g, i)

    def gradient(l, h):
        rows = pl.ds(pl.multiple_of(h * 256, 256), 256)
        return mm3((xh[l], xl[l]), (dh[l, rows], dl[l, rows]), NT)

    lat2_t = lat_t
    scaled = oc[...] * env_t
    delta_t = keep_d(1, 1, scaled * sp[2] + dlat[2] * (spp[2] * update_t[1]))
    h1[0] = gradient(1, 1 - core)
    start_core(0)
    h1[1] = gradient(1, core)

    dlat_t = scaled
    env_rows = [None, None]
    for l in (1, 0):
        if l == 0:
            delta_t = keep_d(0, 1, dlat_t * sp[1] + dlat[1] * (spp[1] * update_t[0]))
            core_to_a(0)
            h2[0] = gradient(0, 1 - core)
            start_core(1)
            h2[1] = gradient(0, core)
        d_inv_t = mm3((latN[l, 0, H:], latN[l, 1, H:]), delta_t)
        d_inv3, d_t, d_w, d_u = kept[l]
        t_t, pr_t = kept_t[l]
        d_inv3_t = jnp.concatenate([d_inv_t] * 3, axis=0)
        d_t_t = d_inv3_t * pp[l] + d_inv3 * pr_t + with_same(d_inv3_t * tt[l] + d_inv3 * t_t)
        ones = jnp.ones((M, E), F32)
        d_w_t = dotted(outer(dir_t, ones), d_t) + dotted(outer(direction, ones), d_t_t)
        d_u_t = split(d_w_t * env + d_w * env_t)
        env_rows[l] = (jnp.concatenate([d_u[0], d_u_t[0]], axis=1), jnp.concatenate([d_u[1], d_u_t[1]], axis=1))
        back = mm3((latN[l, 0, 0:H], latN[l, 1, 0:H]), delta_t) + mm3((envN[l, 0], envN[l, 1]), padded2(d_u_t))
        dlat_t = dlat_t + back
    core_to_a(1)
    keep_d(2, 1, dlat_t * sp[0] + dlat[0] * (spp[0] * first_t))
    feats2 = split(jnp.concatenate([feats_t, feats], axis=1))
    out_sum = split(lat2_t * env + lat[2] * env_t)
    osum[0], osum[1] = out_sum
    ones = jnp.ones((16, E), BF16)

    def rest(h, slot):
        rows = pl.ds(pl.multiple_of(h * 256, 256), 256)
        for l in (1, 0):
            h3[slot, 64 - 64 * l : 128 - 64 * l] = mm3(env_rows[l], (xh[l, rows], xl[l, rows]), NT)
        h3[slot, 128:160] = mm3(feats2, (dh[2, rows], dl[2, rows]), NT)
        o = dot(ones, osum[0, rows], NT) + dot(ones, osum[1, rows], NT)
        h3[slot, 152:160] = o[0:8]
        h3[slot, 160:192] = jnp.zeros((32, 256), F32)

    rest(1 - core, 0)
    start_core(2)
    rest(core, 1)
    step(0, a_to_b)
    core_to_a(2)
    step(1, a_to_b)
    step(0, b_to_c)
    step(2, a_to_b_whole)
    step(1, b_to_c)
    step(0, c_to_b)
    step(2, b_to_c_whole)
    step(1, c_to_b)
    step(0, b_to_a)
    step(2, c_to_a_whole)
    step(1, b_to_a)
    a_to_core(0)
    a_to_core(2)
    a_to_core(1)
    for g in range(3):
        finish(g)
    for c in sends:
        if not any(c is d for d in done):
            c.wait_send()


def unpack(f_ref, g1_ref, g2_ref, g3_ref, forces_ref, rad_ref, cem_ref, nem_ref, env_ref, lat_ref, out_ref):
    lat_ref[1] = g1_ref[...]
    lat_ref[0] = g2_ref[...]
    env_ref[1] = g3_ref[0:64]
    env_ref[0] = g3_ref[64:128]
    rad_ref[...] = g3_ref[128:136]
    cem_ref[...] = g3_ref[136:141]
    nem_ref[...] = g3_ref[144:149]
    out_ref[...] = g3_ref[152:153]
    forces_ref[...] = f_ref[...]


def shape(*dims):
    return jax.ShapeDtypeStruct(dims, F32)


def on_device(
    positions, species, export_index, edge_center, edge_neighbor, edge_count, force_target, radial_weight, center_embed,
    neighbor_embed, environment_weight, latent_weight, output_weight,
):
    vmem = pl.BlockSpec(memory_space=VMEM)
    scratch = [
        VMEM((2, 576, 512), F32),
        VMEM((2, 64, 512), F32),
        VMEM((2, 2, 512, 640), BF16),
        VMEM((2, 2, 576, 512), BF16),
        VMEM((2, 2, 64, 512), BF16),
        VMEM((2, 2, 512, 128), BF16),
        VMEM((32, 512), F32),
        VMEM((H, E), F32),
        VMEM((10, 8, 128), F32),
        VMEM((10, 8, 128), F32),
        VMEM((2, 8, 128), F32),
        VMEM((9, 8, 128), F32),
        VMEM((9, 8, 128), F32),
        VMEM((3, H, E), F32),
        VMEM((2, 576, 512), BF16),
        VMEM((2, 576, 512), BF16),
        VMEM((3, 512, 512), BF16),
        VMEM((3, 512, 512), BF16),
        VMEM((3, H, E), F32),
        VMEM((3, H, E), F32),
        VMEM((3, H, E), F32),
        VMEM((2, H, E), BF16),
        VMEM((2, 3 * M, E), F32),
        VMEM((2, 3 * M, E), F32),
        VMEM((2, M, E), F32),
    ]
    for n in ROWS:
        scratch.append(VMEM((2, n, 256), F32))
    for n in ROWS:
        scratch.append(VMEM((n, 256), F32))
    for n in PARTS:
        scratch.append(VMEM((3, 3, n[0] // 4, 256), F32))
    for _ in (1, 2):
        for n in PARTS[:2]:
            scratch.append(VMEM((3, 3, n[0] // 8, 128), F32))
        scratch.append(VMEM((3, 3, PARTS[2][0] // 4, 256), F32))
    scratch += [
        pltpu.SemaphoreType.DMA((2,)),
        pltpu.SemaphoreType.DMA((3, 8)),
        pltpu.SemaphoreType.DMA((3, 8)),
        pltpu.SemaphoreType.DMA((3, 3, 24)),
        pltpu.SemaphoreType.DMA((3, 3, 24)),
    ]
    any_space = pl.BlockSpec(memory_space=pl.ANY)
    parts = pl.pallas_call(
        kernel,
        out_shape=(VMEM((3, 1, 1, ATOMS), F32),) + tuple(VMEM((n, 512), F32) for n in ROWS),
        in_specs=[vmem] * 11 + [any_space] * 2,
        out_specs=(vmem,) * 4,
        scratch_shapes=scratch,
        compiler_params=pltpu.CompilerParams(collective_id=0, has_side_effects=True, vmem_limit_bytes=56 << 20),
        name="step",
    )(
        positions, species, export_index, edge_center, edge_neighbor, edge_count, force_target, radial_weight, center_embed,
        neighbor_embed, output_weight.reshape(1, 512), jnp.swapaxes(environment_weight, 1, 2), latent_weight,
    )
    outs = pl.pallas_call(
        unpack,
        out_shape=(shape(3, 1, 1, ATOMS), shape(8, 512), shape(5, 512), shape(5, 512), shape(2, 64, 512), shape(2, 576, 512), shape(1, 512)),
        in_specs=[vmem] * 4,
        out_specs=(vmem,) * 7,
        compiler_params=pltpu.CompilerParams(vmem_limit_bytes=32 << 20),
        name="unpack",
    )(*parts)
    forces, radial, near, far, environment, latent, output = outs
    return forces, radial, near, far, jnp.swapaxes(environment, 1, 2), latent, output.reshape(512)


def solution(mesh):
    return jax.shard_map(
        on_device,
        mesh=mesh,
        in_specs=(
            P(None, "slab", "brick", None),
            P("slab", "brick", None),
            P("slab", "brick", None),
            P("slab", "brick", None),
            P("slab", "brick", None),
            P("slab", "brick"),
            P(None, "slab", "brick", None),
            P(),
            P(),
            P(),
            P(),
            P(),
            P(),
        ),
        out_specs=(P(None, "slab", "brick", None), P(), P(), P(), P(), P(), P()),
        check_vma=False,
    )
```

```python
import math

import jax
import jax.numpy as jnp
from jax import lax
from jax.experimental import pallas as pl
from jax.experimental.pallas import tpu as pltpu
from jax.sharding import PartitionSpec as P

F32 = jnp.float32
BF16 = jnp.bfloat16
MESH = pl.DeviceIdType.MESH
VMEM = pltpu.VMEM
NN = (((1,), (0,)), ((), ()))
NT = (((1,), (1,)), ((), ()))
TN = (((0,), (0,)), ((), ()))

cell_width = 1.75
cutoff_radius = 6.0
softening = 0.25

N_SLAB, N_BRICK = 4, 32
H, M, E, ATOMS = 512, 64, 256, 128
ROWS = (576, 576, 192)
PARTS = tuple((n // 3,) * 3 for n in ROWS)
ORDERS = (("x", "y", "z"), ("y", "z", "x"), ("z", "x", "y"))
NEIGHBOURS = [(p, q) for q in (0, 2, 1) for p in (0, 2, 1) if (p, q) != (1, 1)]


def dot(a, b, dims=NN):
    return lax.dot_general(a, b, dims, preferred_element_type=F32)


def split(x):
    high = x.astype(BF16)
    return high, (x - high.astype(F32)).astype(BF16)


def mm3(a, b, dims=NN):
    return dot(a[0], b[0], dims) + (dot(a[0], b[1], dims) + dot(a[1], b[0], dims))


def mm2(a, exact, dims=NN):
    return dot(a[0], exact, dims) + dot(a[1], exact, dims)


def pieces(x):
    a = x.astype(BF16).astype(F32)
    b = (x - a).astype(BF16).astype(F32)
    c = (x - a) - b
    return jnp.concatenate([a, b, c, jnp.zeros_like(x)], axis=0).astype(BF16)


def select(x, hot, dims=NN):
    r = dot(pieces(x), hot, dims)
    return (r[0:8] + r[8:16]) + r[16:24]


def onehot(values, count):
    ids = lax.broadcasted_iota(jnp.int32, (count, values.shape[1]), 0)
    return jnp.where(ids == values, 1.0, 0.0).astype(BF16)


def padded(x):
    return jnp.concatenate([x, jnp.zeros((M, x.shape[1]), x.dtype)], axis=0)


def padded2(x):
    return padded(x[0]), padded(x[1])


def sigmoid(x):
    return 1.0 / (1.0 + jnp.exp(-x))


def device_at(core, x, y, z):
    return (lax.rem(x, 2) * 2 + core, (z * 4 + y) * 2 + lax.div(x, 2))


def kernel(
    pos_in, spec_in, exp_in, cen_in, nbr_in, cnt_ref, tgt_in, rad_in, cem_in, nem_in, ow_in, env_hbm, lat_hbm,
    forces_ref, g1_ref, g2_ref, g3_ref,
    pos_ref, spec_ref, exp_ref, cen_ref, nbr_ref, tgt_ref, rad_ref, cem_ref, nem_ref, ow_ref,
    w_lat, w_env, latT, latN, envT, envN, a0, oc,
    tbl, ttbl, sendbuf, gsend, grecv,
    lat, xh, xl, dh, dl, sp, spp, dlat, osum, tt, pp, uu,
    h1, h2, h3, c1, c2, c3, ra1, ra2, ra3, rb1, rb2, rb3, rc1, rc2, rc3,
    wsem, hs, hr, ars, arr,
):
    s, b = lax.axis_index("slab"), lax.axis_index("brick")
    core, x = lax.rem(s, 2), 2 * lax.rem(b, 2) + lax.div(s, 2)
    y, z = lax.rem(lax.div(b, 2), 4), lax.div(b, 8)
    at = {"x": x, "y": y, "z": z}
    partner = device_at(1 - core, x, y, z)

    def peer(axis, k):
        c = dict(at)
        c[axis] = lax.rem(c[axis] + k, 4)
        return device_at(core, c["x"], c["y"], c["z"])

    def around(p, q):
        return (lax.rem(s + p + N_SLAB - 1, N_SLAB), lax.rem(b + q + N_BRICK - 1, N_BRICK))

    barrier = pltpu.get_barrier_semaphore()
    everyone = [around(p, q) for p, q in NEIGHBOURS] + [partner] + [peer(a, k) for a in "xyz" for k in (1, 2, 3)]
    for d in everyone:
        pl.semaphore_signal(barrier, inc=1, device_id=d, device_id_type=MESH)

    loads = [
        pltpu.make_async_copy(env_hbm, w_env, wsem.at[0]),
        pltpu.make_async_copy(lat_hbm, w_lat, wsem.at[1]),
    ]
    firsts = [
        pltpu.make_async_copy(pos_in, pos_ref, wsem.at[2]),
        pltpu.make_async_copy(spec_in, spec_ref, wsem.at[3]),
        pltpu.make_async_copy(exp_in, exp_ref, wsem.at[4]),
    ]
    loads += [
        pltpu.make_async_copy(cen_in, cen_ref, wsem.at[5]),
        pltpu.make_async_copy(nbr_in, nbr_ref, wsem.at[6]),
        pltpu.make_async_copy(tgt_in, tgt_ref, wsem.at[7]),
        pltpu.make_async_copy(rad_in, rad_ref, wsem.at[8]),
        pltpu.make_async_copy(cem_in, cem_ref, wsem.at[9]),
        pltpu.make_async_copy(nem_in, nem_ref, wsem.at[10]),
        pltpu.make_async_copy(ow_in, ow_ref, wsem.at[11]),
    ]
    for c in firsts + loads:
        c.start()
    for c in firsts:
        c.wait()

    tbl[0] = jnp.zeros((8, ATOMS), F32)
    for m in range(3):
        tbl[0, m : m + 1, :] = pos_ref[m, 0]
    tbl[0, 3:4, :] = spec_ref[0].astype(F32)
    hot_exp = onehot(exp_ref[0], ATOMS)
    sendbuf[0] = select(tbl[0], hot_exp)

    pl.semaphore_wait(barrier, len(everyone))

    def halo(stage, sources, lands, back):
        out = []
        for i, (p, q) in enumerate(NEIGHBOURS):
            k = 3 * p + q
            to = around(p, q) if back else around(2 - p, 2 - q)
            out.append(
                pltpu.make_async_remote_copy(
                    src_ref=sources(k), dst_ref=lands(k), send_sem=hs.at[stage, i], recv_sem=hr.at[stage, i],
                    device_id=to, device_id_type=MESH,
                )
            )
        for c in out:
            c.start()
        return out

    sends = []
    first = halo(0, lambda k: sendbuf.at[0], lambda k: tbl.at[1 + k], False)
    sends += first

    tbl[5] = sendbuf[0]
    for c in loads:
        c.wait()
    center = cen_ref[0]
    hot_c = onehot(center, ATOMS)
    hot_n = onehot(nbr_ref[0], 10 * ATOMS)
    same = dot(hot_c, hot_c, TN).astype(BF16)
    lane = lax.broadcasted_iota(jnp.int32, (1, E), 1)
    live = jnp.where(lane < cnt_ref[...], 1.0, 0.0)
    o_col = jnp.transpose(jnp.broadcast_to(ow_ref[...], (128, H)))
    oc[...] = jnp.concatenate([o_col, o_col], axis=1)
    a0[...] = jnp.zeros_like(a0)
    a0[0:8] = rad_ref[...]
    a0[8:13] = cem_ref[...]
    a0[16:21] = nem_ref[...]
    a0s = split(a0[...])
    for l in range(2):
        w = w_lat[l]
        latN[l, 0], latN[l, 1] = split(w)
        latT[l, 0], latT[l, 1] = split(jnp.transpose(padded(w)))
        w = w_env[l]
        envT[l, 0], envT[l, 1] = split(w)
        envN[l, 0], envN[l, 1] = split(jnp.transpose(padded(w)))

    pc = select(tbl[0], hot_c)

    for c in first:
        c.wait_recv()

    row = lax.broadcasted_iota(jnp.int32, (8, 1), 0)
    blocks = [tbl[0]]
    for p in range(3):
        for q in range(3):
            t = tbl[1 + 3 * p + q]
            if (p, q) != (1, 1):
                cross_z = (lax.div(s + p - 1 + N_SLAB, N_SLAB) - 1).astype(F32) * (N_SLAB * cell_width)
                cross_y = (lax.div(b + q - 1 + N_BRICK, N_BRICK) - 1).astype(F32) * (N_BRICK * cell_width)
                t = t + jnp.where(row == 2, cross_z, 0.0) + jnp.where(row == 1, cross_y, 0.0)
            blocks.append(t)
    pn = select(jnp.concatenate(blocks, axis=1), hot_n)
    vec = jnp.where(row < 3, pn - pc, 0.0)
    squared = jnp.sum(vec * vec, axis=0, keepdims=True) + softening
    dist = jnp.sqrt(squared)
    inv_d = 1.0 / dist
    base = 1.0 - squared / (cutoff_radius * cutoff_radius)
    env = base * base * live
    direction = vec * inv_d
    order = (row + 1).astype(F32) * (math.pi / cutoff_radius)
    angle = order * dist
    sine, cosine = jnp.sin(angle), jnp.cos(angle)
    basis = sine * inv_d
    basis_d = (order * cosine - basis) * inv_d
    hot_sc = jnp.where(row.astype(F32) == pc[3:4], 1.0, 0.0)
    hot_sn = jnp.where(row.astype(F32) == pn[3:4], 1.0, 0.0)
    feats = jnp.concatenate([basis, hot_sc, hot_sn, jnp.zeros((8, E), F32)], axis=0)

    def activation(i, value):
        g = sigmoid(value)
        sp[i] = g * (1.0 + value * (1.0 - g))
        spp[i] = value
        return value * g

    def second_derivative(i):
        value = spp[i]
        g = sigmoid(value)
        spp[i] = (g * (1.0 - g)) * (2.0 + value * (1.0 - 2.0 * g))

    def keep_x(l, half, rows, value):
        high, low = split(value)
        lanes = slice(E * half, E * half + E)
        xh[l, rows, lanes] = high
        xl[l, rows, lanes] = low
        return high, low

    def keep_d(l, half, value):
        high, low = split(value)
        lanes = slice(E * half, E * half + E)
        dh[l, :, lanes] = high
        dl[l, :, lanes] = low
        return high, low

    def thirds(v):
        return [v[m * M : m * M + M] for m in range(3)]

    def outer(d, w):
        return jnp.concatenate([d[m : m + 1] * w for m in range(3)], axis=0)

    def with_same(t):
        return mm2(split(t), same)

    def dotted(a, c):
        r = a * c
        return (r[0:M] + r[M : 2 * M]) + r[2 * M :]

    lat[0] = activation(0, mm3(a0s, split(feats), TN))
    for l in range(2):
        now = keep_x(l, 1, slice(0, H), lat[l])
        u = mm3((envT[l, 0], envT[l, 1]), now)
        uu[l] = u
        t = outer(direction, u * env)
        tt[l] = t
        pr = with_same(t)
        pp[l] = pr
        inv = keep_x(l, 1, slice(H, H + M), dotted(t, pr))
        update = mm3((latT[l, 0, :, 0:H], latT[l, 1, :, 0:H]), now) + mm3((latT[l, 0, :, H:], latT[l, 1, :, H:]), padded2(inv))
        lat[l + 1] = lat[l] + activation(l + 1, update)

    d_env = jnp.sum(oc[...] * lat[2], axis=0, keepdims=True)
    d_dir = [jnp.zeros((1, E), F32) for _ in range(3)]
    dlat[2] = oc[...] * env
    kept = [None, None]
    for l in (1, 0):
        delta = keep_d(l, 0, dlat[l + 1] * sp[l + 1])
        d_inv = mm3((latN[l, 0, H:], latN[l, 1, H:]), delta)
        d_inv3 = jnp.concatenate([d_inv] * 3, axis=0)
        d_t = d_inv3 * pp[l] + with_same(d_inv3 * tt[l])
        w = uu[l] * env
        d_w = dotted(outer(direction, jnp.ones((M, E), F32)), d_t)
        for m, part in enumerate(thirds(d_t)):
            d_dir[m] += jnp.sum(part * w, axis=0, keepdims=True)
        d_env += jnp.sum(d_w * uu[l], axis=0, keepdims=True)
        d_u = split(d_w * env)
        kept[l] = (d_inv3, d_t, d_w, d_u)
        back = mm3((latN[l, 0, 0:H], latN[l, 1, 0:H]), delta) + mm3((envN[l, 0], envN[l, 1]), padded2(d_u))
        dlat[l] = dlat[l + 1] + back
    delta0 = keep_d(2, 0, dlat[0] * sp[0])
    d_basis = mm3(a0s, delta0)[0:8]
    d_dir8 = jnp.concatenate(d_dir + [jnp.zeros((5, E), F32)], axis=0)
    d_dist = jnp.sum(d_basis * basis_d, axis=0, keepdims=True) - jnp.sum(d_dir8 * direction, axis=0, keepdims=True) * inv_d
    base_d = (-2.0 / (cutoff_radius * cutoff_radius)) * base * live
    d_squared = d_env * base_d + d_dist * (0.5 * inv_d)
    d_vec = d_dir8 * inv_d + 2.0 * vec * d_squared
    d_table = select(d_vec, hot_n, NT)
    own = d_table[:, 0:ATOMS] - select(d_vec, hot_c, NT)
    for k in range(9):
        gsend[k] = d_table[:, ATOMS * (k + 1) : ATOMS * (k + 2)]
    second = halo(1, lambda k: gsend.at[k], lambda k: grecv.at[k], True)
    sends += second
    second_derivative(0)
    second_derivative(1)
    for c in second:
        c.wait_recv()
    returned = gsend[4]
    for p, q in NEIGHBOURS:
        returned = returned + grecv[3 * p + q]
    total = own + select(returned, hot_exp, NT)
    ttbl[0] = jnp.zeros((8, ATOMS), F32)
    for m in range(3):
        forces_ref[m, 0] = -total[m : m + 1]
        ttbl[0, m : m + 1, :] = (2.0 / (3.0 * ATOMS)) * (total[m : m + 1] + tgt_ref[m, 0])

    sendbuf[1] = select(ttbl[0], hot_exp)
    third = halo(2, lambda k: sendbuf.at[1], lambda k: ttbl.at[1 + k], False)
    sends += third
    ttbl[5] = sendbuf[1]
    second_derivative(2)
    vc = select(ttbl[0], hot_c)
    for c in third:
        c.wait_recv()
    vn = select(jnp.concatenate([ttbl[k] for k in range(10)], axis=1), hot_n)
    vec_t = vn - vc
    dist_t = jnp.sum(vec * vec_t, axis=0, keepdims=True) * inv_d
    env_t = (2.0 * base_d) * (dist * dist_t)
    dir_t = (vec_t - direction * dist_t) * inv_d
    basis_t = basis_d * dist_t
    feats_t = jnp.concatenate([basis_t, jnp.zeros((24, E), F32)], axis=0)

    first_t = mm3(a0s, split(feats_t), TN)
    lat_t = sp[0] * first_t
    kept_t = [None, None]
    update_t = [None, None]
    for l in range(2):
        now = keep_x(l, 0, slice(0, H), lat_t)
        u_t = mm3((envT[l, 0], envT[l, 1]), now)
        w = uu[l] * env
        w_t = u_t * env + uu[l] * env_t
        t_t = outer(dir_t, w) + outer(direction, w_t)
        pr_t = with_same(t_t)
        inv_t = keep_x(l, 0, slice(H, H + M), dotted(t_t, pp[l]) + dotted(tt[l], pr_t))
        kept_t[l] = (t_t, pr_t)
        update_t[l] = mm3((latT[l, 0, :, 0:H], latT[l, 1, :, 0:H]), now) + mm3((latT[l, 0, :, H:], latT[l, 1, :, H:]), padded2(inv_t))
        lat_t = lat_t + sp[l + 1] * update_t[l]

    half = (h1, h2, h3)
    from_core = (c1, c2, c3)
    from_a, from_b, from_c = (ra1, ra2, ra3), (rb1, rb2, rb3), (rc1, rc2, rc3)
    result = (g1_ref, g2_ref, g3_ref)
    flying, done = {}, []

    def place(g, i):
        n = PARTS[g][i]
        row0 = sum(PARTS[g][:i])
        a, bb, c = ORDERS[i]
        row_a = row0 + at[a] * (n // 4)
        row_b = row_a + lax.div(at[bb], 2) * (n // 8)
        return n, row0, a, bb, c, pl.multiple_of(row_a, 8), pl.multiple_of(row_b, 8)

    def piece_of(row_a, n, where):
        rows = pl.ds(pl.multiple_of(row_a + lax.div(where, 2) * (n // 8), 8), n // 8)
        return rows, lax.rem(where, 2) * 128

    def copy(g, i, j, src, dst, to):
        c = pltpu.make_async_remote_copy(
            src_ref=src, dst_ref=dst, send_sem=ars.at[g, i, j], recv_sem=arr.at[g, i, j], device_id=to, device_id_type=MESH
        )
        c.start()
        sends.append(c)
        flying[g, i, j] = c

    def lands(g, i, j):
        flying[g, i, j].wait_recv()

    def lanes_at(first, count=128):
        return pl.ds(pl.multiple_of(first, 128), count)

    def chunk(g, i, k):
        n, row0, a, *_ = place(g, i)
        return pl.ds(pl.multiple_of(row0 + lax.rem(at[a] + k, 4) * (n // 4), 8), n // 4)

    def start_core(g):
        for k in (2, 1, 3, 0):
            for i in range(3):
                rows = chunk(g, i, k)
                copy(g, i, 16 + k, half[g].at[0, rows], from_core[g].at[rows], partner)

    def core_to_a(g):
        for k in (2, 1, 3, 0):
            for i in range(3):
                lands(g, i, 16 + k)
                rows = chunk(g, i, k)
                half[g][1, rows] = half[g][1, rows] + from_core[g][rows]
                if k:
                    a = ORDERS[i][0]
                    copy(g, i, k, half[g].at[1, rows], from_a[g].at[i, k - 1], peer(a, k))

    def a_to_b(g, i):
        n, row0, a, bb, c, row_a, row_b = place(g, i)
        for k in (1, 2, 3):
            lands(g, i, k)
        rows = pl.ds(row_a, n // 4)
        half[g][1, rows] = (half[g][1, rows] + from_a[g][i, 1]) + (from_a[g][i, 0] + from_a[g][i, 2])
        for k in (1, 2, 3):
            rows, lane0 = piece_of(row_a, n, lax.rem(at[bb] + k, 4))
            copy(g, i, 3 + k, half[g].at[1, rows, lanes_at(lane0)], from_b[g].at[i, k - 1], peer(bb, k))

    def b_to_c(g, i):
        n, row0, a, bb, c, row_a, row_b = place(g, i)
        for k in (1, 2, 3):
            lands(g, i, 3 + k)
        rows, lane0 = piece_of(row_a, n, at[bb])
        lanes = lanes_at(lane0)
        half[g][1, rows, lanes] = (half[g][1, rows, lanes] + from_b[g][i, 1]) + (from_b[g][i, 0] + from_b[g][i, 2])
        for k in (1, 2, 3):
            copy(g, i, 6 + k, half[g].at[1, rows, lanes], from_c[g].at[i, k - 1], peer(c, k))

    def c_to_b(g, i):
        n, row0, a, bb, c, row_a, row_b = place(g, i)
        for k in (1, 2, 3):
            lands(g, i, 6 + k)
        rows, lane0 = piece_of(row_a, n, at[bb])
        mine = half[g][1, rows, lanes_at(lane0)]
        out = lanes_at(core * 256 + lane0)
        result[g][rows, out] = (mine + from_c[g][i, 1]) + (from_c[g][i, 0] + from_c[g][i, 2])
        for k in (1, 2, 3):
            here = result[g].at[rows, out]
            copy(g, i, 9 + k, here, here, peer(bb, k))

    def b_to_a(g, i):
        n, row0, a, bb, c, row_a, row_b = place(g, i)
        for k in (1, 2, 3):
            lands(g, i, 9 + k)
        here = result[g].at[pl.ds(row_a, n // 4), lanes_at(core * 256, 256)]
        for k in (2, 1, 3):
            copy(g, i, 12 + k, here, here, peer(a, k))
        copy(g, i, 20, here, here, partner)

    def a_to_core(g):
        for k in (1, 3, 2):
            for i in range(3):
                lands(g, i, 12 + k)
                here = result[g].at[chunk(g, i, 4 - k), lanes_at(core * 256, 256)]
                copy(g, i, 20 + k, here, here, partner)

    def finish(g):
        for i in range(3):
            for k in range(4):
                lands(g, i, 20 + k)

    def whole_chunk(g, i):
        row_a = place(g, i)[5]
        return half[g].at[1, pl.ds(row_a, PARTS[g][i] // 4)]

    def exchange(g, i, first, came_from, axis):
        here = whole_chunk(g, i)
        for k in (2, 1, 3):
            copy(g, i, first + k, here, came_from[g].at[i, k - 1], peer(axis, k))

    def a_to_b_whole(g, i):
        for k in (1, 2, 3):
            lands(g, i, k)
        here = whole_chunk(g, i)
        here[...] = (here[...] + from_a[g][i, 1]) + (from_a[g][i, 0] + from_a[g][i, 2])
        exchange(g, i, 3, from_b, ORDERS[i][1])

    def b_to_c_whole(g, i):
        for k in (1, 2, 3):
            lands(g, i, 3 + k)
            flying[g, i, 3 + k].wait_send()
            done.append(flying[g, i, 3 + k])
        here = whole_chunk(g, i)
        here[...] = (here[...] + from_b[g][i, 1]) + (from_b[g][i, 0] + from_b[g][i, 2])
        exchange(g, i, 6, from_c, ORDERS[i][2])

    def c_to_a_whole(g, i):
        for k in (1, 2, 3):
            lands(g, i, 6 + k)
        n, row0, a, bb, c, row_a, row_b = place(g, i)
        out = result[g].at[pl.ds(row_a, n // 4), lanes_at(core * 256, 256)]
        here = whole_chunk(g, i)
        out[...] = (here[...] + from_c[g][i, 1]) + (from_c[g][i, 0] + from_c[g][i, 2])
        for k in (2, 1, 3):
            copy(g, i, 12 + k, out, out, peer(a, k))
        copy(g, i, 20, out, out, partner)

    def step(g, f):
        for i in range(3):
            f(g, i)

    def gradient(l, h):
        rows = pl.ds(pl.multiple_of(h * 256, 256), 256)
        return mm3((xh[l], xl[l]), (dh[l, rows], dl[l, rows]), NT)

    lat2_t = lat_t
    scaled = oc[...] * env_t
    delta_t = keep_d(1, 1, scaled * sp[2] + dlat[2] * (spp[2] * update_t[1]))
    h1[0] = gradient(1, 1 - core)
    start_core(0)
    h1[1] = gradient(1, core)

    dlat_t = scaled
    env_rows = [None, None]
    for l in (1, 0):
        if l == 0:
            delta_t = keep_d(0, 1, dlat_t * sp[1] + dlat[1] * (spp[1] * update_t[0]))
            core_to_a(0)
            h2[0] = gradient(0, 1 - core)
            start_core(1)
            h2[1] = gradient(0, core)
        d_inv_t = mm3((latN[l, 0, H:], latN[l, 1, H:]), delta_t)
        d_inv3, d_t, d_w, d_u = kept[l]
        t_t, pr_t = kept_t[l]
        d_inv3_t = jnp.concatenate([d_inv_t] * 3, axis=0)
        d_t_t = d_inv3_t * pp[l] + d_inv3 * pr_t + with_same(d_inv3_t * tt[l] + d_inv3 * t_t)
        ones = jnp.ones((M, E), F32)
        d_w_t = dotted(outer(dir_t, ones), d_t) + dotted(outer(direction, ones), d_t_t)
        d_u_t = split(d_w_t * env + d_w * env_t)
        env_rows[l] = (jnp.concatenate([d_u[0], d_u_t[0]], axis=1), jnp.concatenate([d_u[1], d_u_t[1]], axis=1))
        back = mm3((latN[l, 0, 0:H], latN[l, 1, 0:H]), delta_t) + mm3((envN[l, 0], envN[l, 1]), padded2(d_u_t))
        dlat_t = dlat_t + back
    core_to_a(1)
    keep_d(2, 1, dlat_t * sp[0] + dlat[0] * (spp[0] * first_t))
    feats2 = split(jnp.concatenate([feats_t, feats], axis=1))
    out_sum = split(lat2_t * env + lat[2] * env_t)
    osum[0], osum[1] = out_sum
    ones = jnp.ones((16, E), BF16)

    def rest(h, slot):
        rows = pl.ds(pl.multiple_of(h * 256, 256), 256)
        for l in (1, 0):
            h3[slot, 64 - 64 * l : 128 - 64 * l] = mm3(env_rows[l], (xh[l, rows], xl[l, rows]), NT)
        h3[slot, 128:160] = mm3(feats2, (dh[2, rows], dl[2, rows]), NT)
        o = dot(ones, osum[0, rows], NT) + dot(ones, osum[1, rows], NT)
        h3[slot, 152:160] = o[0:8]
        h3[slot, 160:192] = jnp.zeros((32, 256), F32)

    rest(1 - core, 0)
    start_core(2)
    rest(core, 1)
    step(0, a_to_b)
    core_to_a(2)
    step(1, a_to_b_whole)
    step(0, b_to_c)
    step(2, a_to_b_whole)
    step(1, b_to_c_whole)
    step(0, c_to_b)
    step(2, b_to_c_whole)
    step(1, c_to_a_whole)
    step(0, b_to_a)
    step(2, c_to_a_whole)
    a_to_core(1)
    a_to_core(0)
    a_to_core(2)
    for g in range(3):
        finish(g)
    for c in sends:
        if not any(c is d for d in done):
            c.wait_send()


def unpack(f_ref, g1_ref, g2_ref, g3_ref, forces_ref, rad_ref, cem_ref, nem_ref, env_ref, lat_ref, out_ref):
    lat_ref[1] = g1_ref[...]
    lat_ref[0] = g2_ref[...]
    env_ref[1] = g3_ref[0:64]
    env_ref[0] = g3_ref[64:128]
    rad_ref[...] = g3_ref[128:136]
    cem_ref[...] = g3_ref[136:141]
    nem_ref[...] = g3_ref[144:149]
    out_ref[...] = g3_ref[152:153]
    forces_ref[...] = f_ref[...]


def shape(*dims):
    return jax.ShapeDtypeStruct(dims, F32)


def on_device(
    positions, species, export_index, edge_center, edge_neighbor, edge_count, force_target, radial_weight, center_embed,
    neighbor_embed, environment_weight, latent_weight, output_weight,
):
    vmem = pl.BlockSpec(memory_space=VMEM)
    scratch = [
        VMEM((3, 1, 1, ATOMS), F32),
        VMEM((1, 1, ATOMS), jnp.int32),
        VMEM((1, 1, ATOMS), jnp.int32),
        VMEM((1, 1, E), jnp.int32),
        VMEM((1, 1, E), jnp.int32),
        VMEM((3, 1, 1, ATOMS), F32),
        VMEM((8, H), F32),
        VMEM((5, H), F32),
        VMEM((5, H), F32),
        VMEM((1, H), F32),
        VMEM((2, 576, 512), F32),
        VMEM((2, 64, 512), F32),
        VMEM((2, 2, 512, 640), BF16),
        VMEM((2, 2, 576, 512), BF16),
        VMEM((2, 2, 64, 512), BF16),
        VMEM((2, 2, 512, 128), BF16),
        VMEM((32, 512), F32),
        VMEM((H, E), F32),
        VMEM((10, 8, 128), F32),
        VMEM((10, 8, 128), F32),
        VMEM((2, 8, 128), F32),
        VMEM((9, 8, 128), F32),
        VMEM((9, 8, 128), F32),
        VMEM((3, H, E), F32),
        VMEM((2, 576, 512), BF16),
        VMEM((2, 576, 512), BF16),
        VMEM((3, 512, 512), BF16),
        VMEM((3, 512, 512), BF16),
        VMEM((3, H, E), F32),
        VMEM((3, H, E), F32),
        VMEM((3, H, E), F32),
        VMEM((2, H, E), BF16),
        VMEM((2, 3 * M, E), F32),
        VMEM((2, 3 * M, E), F32),
        VMEM((2, M, E), F32),
    ]
    for n in ROWS:
        scratch.append(VMEM((2, n, 256), F32))
    for n in ROWS:
        scratch.append(VMEM((n, 256), F32))
    for n in PARTS:
        scratch.append(VMEM((3, 3, n[0] // 4, 256), F32))
    for _ in (1, 2):
        for g, n in enumerate(PARTS):
            scratch.append(VMEM((3, 3) + ((n[0] // 4, 256) if g in (1, 2) else (n[0] // 8, 128)), F32))
    scratch += [
        pltpu.SemaphoreType.DMA((12,)),
        pltpu.SemaphoreType.DMA((3, 8)),
        pltpu.SemaphoreType.DMA((3, 8)),
        pltpu.SemaphoreType.DMA((3, 3, 24)),
        pltpu.SemaphoreType.DMA((3, 3, 24)),
    ]
    any_space = pl.BlockSpec(memory_space=pl.ANY)
    parts = pl.pallas_call(
        kernel,
        out_shape=(VMEM((3, 1, 1, ATOMS), F32),) + tuple(VMEM((n, 512), F32) for n in ROWS),
        in_specs=[any_space] * 5 + [vmem] + [any_space] * 7,
        out_specs=(vmem,) * 4,
        scratch_shapes=scratch,
        compiler_params=pltpu.CompilerParams(collective_id=0, has_side_effects=True, vmem_limit_bytes=56 << 20),
        name="step",
    )(
        positions, species, export_index, edge_center, edge_neighbor, edge_count, force_target, radial_weight, center_embed,
        neighbor_embed, output_weight.reshape(1, 512), jnp.swapaxes(environment_weight, 1, 2), latent_weight,
    )
    outs = pl.pallas_call(
        unpack,
        out_shape=(shape(3, 1, 1, ATOMS), shape(8, 512), shape(5, 512), shape(5, 512), shape(2, 64, 512), shape(2, 576, 512), shape(1, 512)),
        in_specs=[vmem] * 4,
        out_specs=(vmem,) * 7,
        compiler_params=pltpu.CompilerParams(vmem_limit_bytes=32 << 20),
        name="unpack",
    )(*parts)
    forces, radial, near, far, environment, latent, output = outs
    return forces, radial, near, far, jnp.swapaxes(environment, 1, 2), latent, output.reshape(512)


def solution(mesh):
    return jax.shard_map(
        on_device,
        mesh=mesh,
        in_specs=(
            P(None, "slab", "brick", None),
            P("slab", "brick", None),
            P("slab", "brick", None),
            P("slab", "brick", None),
            P("slab", "brick", None),
            P("slab", "brick"),
            P(None, "slab", "brick", None),
            P(),
            P(),
            P(),
            P(),
            P(),
            P(),
        ),
        out_specs=(P(None, "slab", "brick", None), P(), P(), P(), P(), P(), P()),
        check_vma=False,
    )
```

```python
import math

import jax
import jax.numpy as jnp
from jax import lax
from jax.experimental import pallas as pl
from jax.experimental.pallas import tpu as pltpu
from jax.sharding import PartitionSpec as P

F32 = jnp.float32
BF16 = jnp.bfloat16
MESH = pl.DeviceIdType.MESH
VMEM = pltpu.VMEM
NN = (((1,), (0,)), ((), ()))
NT = (((1,), (1,)), ((), ()))
TN = (((0,), (0,)), ((), ()))

cell_width = 1.75
cutoff_radius = 6.0
softening = 0.25

N_SLAB, N_BRICK = 4, 32
H, M, E, ATOMS = 512, 64, 256, 128
ROWS = (576, 576, 192)
PARTS = tuple((n // 3,) * 3 for n in ROWS)
ORDERS = (("x", "y", "z"), ("y", "z", "x"), ("z", "x", "y"))
NEIGHBOURS = [(p, q) for q in (0, 2, 1) for p in (0, 2, 1) if (p, q) != (1, 1)]


def dot(a, b, dims=NN):
    return lax.dot_general(a, b, dims, preferred_element_type=F32)


def split(x):
    high = x.astype(BF16)
    return high, (x - high.astype(F32)).astype(BF16)


def mm3(a, b, dims=NN):
    return dot(a[0], b[0], dims) + (dot(a[0], b[1], dims) + dot(a[1], b[0], dims))


def mm2(a, exact, dims=NN):
    return dot(a[0], exact, dims) + dot(a[1], exact, dims)


def pieces(x):
    a = x.astype(BF16).astype(F32)
    b = (x - a).astype(BF16).astype(F32)
    c = (x - a) - b
    return jnp.concatenate([a, b, c, jnp.zeros_like(x)], axis=0).astype(BF16)


def select(x, hot, dims=NN):
    r = dot(pieces(x), hot, dims)
    return (r[0:8] + r[8:16]) + r[16:24]


def onehot(values, count):
    ids = lax.broadcasted_iota(jnp.int32, (count, values.shape[1]), 0)
    return jnp.where(ids == values, 1.0, 0.0).astype(BF16)


def padded(x):
    return jnp.concatenate([x, jnp.zeros((M, x.shape[1]), x.dtype)], axis=0)


def padded2(x):
    return padded(x[0]), padded(x[1])


def sigmoid(x):
    return 0.5 + 0.5 * jnp.tanh(0.5 * x)


def device_at(core, x, y, z):
    return (lax.rem(x, 2) * 2 + core, (z * 4 + y) * 2 + lax.div(x, 2))


def kernel(
    pos_in, spec_in, exp_in, cen_in, nbr_in, cnt_ref, tgt_in, rad_in, cem_in, nem_in, ow_in, env_hbm, lat_hbm,
    forces_ref, g1_ref, g2_ref, g3_ref,
    pos_ref, spec_ref, exp_ref, cen_ref, nbr_ref, tgt_ref, rad_ref, cem_ref, nem_ref, ow_ref,
    w_lat, w_env, latT, latN, envT, envN, a0, oc,
    tbl, ttbl, sendbuf, gsend, grecv,
    lat, xh, xl, dh, dl, sp, spp, dlat, osum, tt, pp, uu,
    h1, h2, h3, c1, c2, c3, ra1, ra2, ra3, rb1, rb2, rb3, rc1, rc2, rc3,
    wsem, hs, hr, ars, arr,
):
    s, b = lax.axis_index("slab"), lax.axis_index("brick")
    core, x = lax.rem(s, 2), 2 * lax.rem(b, 2) + lax.div(s, 2)
    y, z = lax.rem(lax.div(b, 2), 4), lax.div(b, 8)
    at = {"x": x, "y": y, "z": z}
    partner = device_at(1 - core, x, y, z)

    def peer(axis, k):
        c = dict(at)
        c[axis] = lax.rem(c[axis] + k, 4)
        return device_at(core, c["x"], c["y"], c["z"])

    def around(p, q):
        return (lax.rem(s + p + N_SLAB - 1, N_SLAB), lax.rem(b + q + N_BRICK - 1, N_BRICK))

    barrier = pltpu.get_barrier_semaphore()
    everyone = [around(p, q) for p, q in NEIGHBOURS] + [partner] + [peer(a, k) for a in "xyz" for k in (1, 2, 3)]
    for d in everyone:
        pl.semaphore_signal(barrier, inc=1, device_id=d, device_id_type=MESH)

    loads = [
        pltpu.make_async_copy(env_hbm, w_env, wsem.at[0]),
        pltpu.make_async_copy(lat_hbm, w_lat, wsem.at[1]),
    ]
    firsts = [
        pltpu.make_async_copy(pos_in, pos_ref, wsem.at[2]),
        pltpu.make_async_copy(spec_in, spec_ref, wsem.at[3]),
        pltpu.make_async_copy(exp_in, exp_ref, wsem.at[4]),
    ]
    loads += [
        pltpu.make_async_copy(cen_in, cen_ref, wsem.at[5]),
        pltpu.make_async_copy(nbr_in, nbr_ref, wsem.at[6]),
        pltpu.make_async_copy(tgt_in, tgt_ref, wsem.at[7]),
        pltpu.make_async_copy(rad_in, rad_ref, wsem.at[8]),
        pltpu.make_async_copy(cem_in, cem_ref, wsem.at[9]),
        pltpu.make_async_copy(nem_in, nem_ref, wsem.at[10]),
        pltpu.make_async_copy(ow_in, ow_ref, wsem.at[11]),
    ]
    for c in firsts + loads:
        c.start()
    for c in firsts:
        c.wait()

    tbl[0] = jnp.zeros((8, ATOMS), F32)
    for m in range(3):
        tbl[0, m : m + 1, :] = pos_ref[m, 0]
    tbl[0, 3:4, :] = spec_ref[0].astype(F32)
    hot_exp = onehot(exp_ref[0], ATOMS)
    sendbuf[0] = select(tbl[0], hot_exp)

    pl.semaphore_wait(barrier, len(everyone))

    def halo(stage, sources, lands, back):
        out = []
        for i, (p, q) in enumerate(NEIGHBOURS):
            k = 3 * p + q
            to = around(p, q) if back else around(2 - p, 2 - q)
            out.append(
                pltpu.make_async_remote_copy(
                    src_ref=sources(k), dst_ref=lands(k), send_sem=hs.at[stage, i], recv_sem=hr.at[stage, i],
                    device_id=to, device_id_type=MESH,
                )
            )
        for c in out:
            c.start()
        return out

    sends = []
    first = halo(0, lambda k: sendbuf.at[0], lambda k: tbl.at[1 + k], False)
    sends += first

    tbl[5] = sendbuf[0]
    for c in loads:
        c.wait()
    center = cen_ref[0]
    hot_c = onehot(center, ATOMS)
    hot_n = onehot(nbr_ref[0], 10 * ATOMS)
    same = dot(hot_c, hot_c, TN).astype(BF16)
    lane = lax.broadcasted_iota(jnp.int32, (1, E), 1)
    live = jnp.where(lane < cnt_ref[...], 1.0, 0.0)
    o_col = jnp.transpose(jnp.broadcast_to(ow_ref[...], (128, H)))
    oc[...] = jnp.concatenate([o_col, o_col], axis=1)
    a0[...] = jnp.zeros_like(a0)
    a0[0:8] = rad_ref[...]
    a0[8:13] = cem_ref[...]
    a0[16:21] = nem_ref[...]
    a0s = split(a0[...])
    for l in range(2):
        w = w_lat[l]
        latN[l, 0], latN[l, 1] = split(w)
        latT[l, 0], latT[l, 1] = split(jnp.transpose(padded(w)))
        w = w_env[l]
        envT[l, 0], envT[l, 1] = split(w)
        envN[l, 0], envN[l, 1] = split(jnp.transpose(padded(w)))

    pc = select(tbl[0], hot_c)

    for c in first:
        c.wait_recv()

    row = lax.broadcasted_iota(jnp.int32, (8, 1), 0)
    blocks = [tbl[0]]
    for p in range(3):
        for q in range(3):
            t = tbl[1 + 3 * p + q]
            if (p, q) != (1, 1):
                cross_z = (lax.div(s + p - 1 + N_SLAB, N_SLAB) - 1).astype(F32) * (N_SLAB * cell_width)
                cross_y = (lax.div(b + q - 1 + N_BRICK, N_BRICK) - 1).astype(F32) * (N_BRICK * cell_width)
                t = t + jnp.where(row == 2, cross_z, 0.0) + jnp.where(row == 1, cross_y, 0.0)
            blocks.append(t)
    pn = select(jnp.concatenate(blocks, axis=1), hot_n)
    vec = jnp.where(row < 3, pn - pc, 0.0)
    squared = jnp.sum(vec * vec, axis=0, keepdims=True) + softening
    dist = jnp.sqrt(squared)
    inv_d = 1.0 / dist
    base = 1.0 - squared / (cutoff_radius * cutoff_radius)
    env = base * base * live
    direction = vec * inv_d
    order = (row + 1).astype(F32) * (math.pi / cutoff_radius)
    angle = order * dist
    sine, cosine = jnp.sin(angle), jnp.cos(angle)
    basis = sine * inv_d
    basis_d = (order * cosine - basis) * inv_d
    hot_sc = jnp.where(row.astype(F32) == pc[3:4], 1.0, 0.0)
    hot_sn = jnp.where(row.astype(F32) == pn[3:4], 1.0, 0.0)
    feats = jnp.concatenate([basis, hot_sc, hot_sn, jnp.zeros((8, E), F32)], axis=0)

    def activation(i, value):
        g = sigmoid(value)
        sp[i] = g * (1.0 + value * (1.0 - g))
        spp[i] = value
        return value * g

    def second_derivative(i):
        value = spp[i]
        g = sigmoid(value)
        spp[i] = (g * (1.0 - g)) * (2.0 + value * (1.0 - 2.0 * g))

    def keep_x(l, half, rows, value):
        high, low = split(value)
        lanes = slice(E * half, E * half + E)
        xh[l, rows, lanes] = high
        xl[l, rows, lanes] = low
        return high, low

    def keep_d(l, half, value):
        high, low = split(value)
        lanes = slice(E * half, E * half + E)
        dh[l, :, lanes] = high
        dl[l, :, lanes] = low
        return high, low

    def thirds(v):
        return [v[m * M : m * M + M] for m in range(3)]

    def outer(d, w):
        return jnp.concatenate([d[m : m + 1] * w for m in range(3)], axis=0)

    def with_same(t):
        return mm2(split(t), same)

    def dotted(a, c):
        r = a * c
        return (r[0:M] + r[M : 2 * M]) + r[2 * M :]

    lat[0] = activation(0, mm3(a0s, split(feats), TN))
    for l in range(2):
        now = keep_x(l, 1, slice(0, H), lat[l])
        u = mm3((envT[l, 0], envT[l, 1]), now)
        uu[l] = u
        t = outer(direction, u * env)
        tt[l] = t
        pr = with_same(t)
        pp[l] = pr
        inv = keep_x(l, 1, slice(H, H + M), dotted(t, pr))
        update = mm3((latT[l, 0, :, 0:H], latT[l, 1, :, 0:H]), now) + mm3((latT[l, 0, :, H:], latT[l, 1, :, H:]), padded2(inv))
        lat[l + 1] = lat[l] + activation(l + 1, update)

    d_env = jnp.sum(oc[...] * lat[2], axis=0, keepdims=True)
    d_dir = [jnp.zeros((1, E), F32) for _ in range(3)]
    dlat[2] = oc[...] * env
    kept = [None, None]
    for l in (1, 0):
        delta = keep_d(l, 0, dlat[l + 1] * sp[l + 1])
        d_inv = mm3((latN[l, 0, H:], latN[l, 1, H:]), delta)
        d_inv3 = jnp.concatenate([d_inv] * 3, axis=0)
        d_t = d_inv3 * pp[l] + with_same(d_inv3 * tt[l])
        w = uu[l] * env
        d_w = dotted(outer(direction, jnp.ones((M, E), F32)), d_t)
        for m, part in enumerate(thirds(d_t)):
            d_dir[m] += jnp.sum(part * w, axis=0, keepdims=True)
        d_env += jnp.sum(d_w * uu[l], axis=0, keepdims=True)
        d_u = split(d_w * env)
        kept[l] = (d_inv3, d_t, d_w, d_u)
        back = mm3((latN[l, 0, 0:H], latN[l, 1, 0:H]), delta) + mm3((envN[l, 0], envN[l, 1]), padded2(d_u))
        dlat[l] = dlat[l + 1] + back
    delta0 = keep_d(2, 0, dlat[0] * sp[0])
    d_basis = mm3(a0s, delta0)[0:8]
    d_dir8 = jnp.concatenate(d_dir + [jnp.zeros((5, E), F32)], axis=0)
    d_dist = jnp.sum(d_basis * basis_d, axis=0, keepdims=True) - jnp.sum(d_dir8 * direction, axis=0, keepdims=True) * inv_d
    base_d = (-2.0 / (cutoff_radius * cutoff_radius)) * base * live
    d_squared = d_env * base_d + d_dist * (0.5 * inv_d)
    d_vec = d_dir8 * inv_d + 2.0 * vec * d_squared
    d_table = select(d_vec, hot_n, NT)
    own = d_table[:, 0:ATOMS] - select(d_vec, hot_c, NT)
    for k in range(9):
        gsend[k] = d_table[:, ATOMS * (k + 1) : ATOMS * (k + 2)]
    second = halo(1, lambda k: gsend.at[k], lambda k: grecv.at[k], True)
    sends += second
    second_derivative(0)
    second_derivative(1)
    for c in second:
        c.wait_recv()
    returned = gsend[4]
    for p, q in NEIGHBOURS:
        returned = returned + grecv[3 * p + q]
    total = own + select(returned, hot_exp, NT)
    ttbl[0] = jnp.zeros((8, ATOMS), F32)
    for m in range(3):
        forces_ref[m, 0] = -total[m : m + 1]
        ttbl[0, m : m + 1, :] = (2.0 / (3.0 * ATOMS)) * (total[m : m + 1] + tgt_ref[m, 0])

    sendbuf[1] = select(ttbl[0], hot_exp)
    third = halo(2, lambda k: sendbuf.at[1], lambda k: ttbl.at[1 + k], False)
    sends += third
    ttbl[5] = sendbuf[1]
    second_derivative(2)
    vc = select(ttbl[0], hot_c)
    for c in third:
        c.wait_recv()
    vn = select(jnp.concatenate([ttbl[k] for k in range(10)], axis=1), hot_n)
    vec_t = vn - vc
    dist_t = jnp.sum(vec * vec_t, axis=0, keepdims=True) * inv_d
    env_t = (2.0 * base_d) * (dist * dist_t)
    dir_t = (vec_t - direction * dist_t) * inv_d
    basis_t = basis_d * dist_t
    feats_t = jnp.concatenate([basis_t, jnp.zeros((24, E), F32)], axis=0)

    first_t = mm3(a0s, split(feats_t), TN)
    lat_t = sp[0] * first_t
    kept_t = [None, None]
    update_t = [None, None]
    for l in range(2):
        now = keep_x(l, 0, slice(0, H), lat_t)
        u_t = mm3((envT[l, 0], envT[l, 1]), now)
        w = uu[l] * env
        w_t = u_t * env + uu[l] * env_t
        t_t = outer(dir_t, w) + outer(direction, w_t)
        pr_t = with_same(t_t)
        inv_t = keep_x(l, 0, slice(H, H + M), dotted(t_t, pp[l]) + dotted(tt[l], pr_t))
        kept_t[l] = (t_t, pr_t)
        update_t[l] = mm3((latT[l, 0, :, 0:H], latT[l, 1, :, 0:H]), now) + mm3((latT[l, 0, :, H:], latT[l, 1, :, H:]), padded2(inv_t))
        lat_t = lat_t + sp[l + 1] * update_t[l]

    half = (h1, h2, h3)
    from_core = (c1, c2, c3)
    from_a, from_b, from_c = (ra1, ra2, ra3), (rb1, rb2, rb3), (rc1, rc2, rc3)
    result = (g1_ref, g2_ref, g3_ref)
    flying, done = {}, []

    def place(g, i):
        n = PARTS[g][i]
        row0 = sum(PARTS[g][:i])
        a, bb, c = ORDERS[i]
        row_a = row0 + at[a] * (n // 4)
        row_b = row_a + lax.div(at[bb], 2) * (n // 8)
        return n, row0, a, bb, c, pl.multiple_of(row_a, 8), pl.multiple_of(row_b, 8)

    def piece_of(row_a, n, where):
        rows = pl.ds(pl.multiple_of(row_a + lax.div(where, 2) * (n // 8), 8), n // 8)
        return rows, lax.rem(where, 2) * 128

    def copy(g, i, j, src, dst, to):
        c = pltpu.make_async_remote_copy(
            src_ref=src, dst_ref=dst, send_sem=ars.at[g, i, j], recv_sem=arr.at[g, i, j], device_id=to, device_id_type=MESH
        )
        c.start()
        sends.append(c)
        flying[g, i, j] = c

    def lands(g, i, j):
        flying[g, i, j].wait_recv()

    def lanes_at(first, count=128):
        return pl.ds(pl.multiple_of(first, 128), count)

    def chunk(g, i, k):
        n, row0, a, *_ = place(g, i)
        return pl.ds(pl.multiple_of(row0 + lax.rem(at[a] + k, 4) * (n // 4), 8), n // 4)

    def start_core(g):
        for k in (2, 1, 3, 0):
            for i in range(3):
                rows = chunk(g, i, k)
                copy(g, i, 16 + k, half[g].at[0, rows], from_core[g].at[rows], partner)

    def core_to_a(g):
        for k in (2, 1, 3, 0):
            for i in range(3):
                lands(g, i, 16 + k)
                rows = chunk(g, i, k)
                half[g][1, rows] = half[g][1, rows] + from_core[g][rows]
                if k:
                    a = ORDERS[i][0]
                    copy(g, i, k, half[g].at[1, rows], from_a[g].at[i, k - 1], peer(a, k))

    def a_to_b(g, i):
        n, row0, a, bb, c, row_a, row_b = place(g, i)
        for k in (1, 2, 3):
            lands(g, i, k)
        rows = pl.ds(row_a, n // 4)
        half[g][1, rows] = (half[g][1, rows] + from_a[g][i, 1]) + (from_a[g][i, 0] + from_a[g][i, 2])
        for k in (1, 2, 3):
            rows, lane0 = piece_of(row_a, n, lax.rem(at[bb] + k, 4))
            copy(g, i, 3 + k, half[g].at[1, rows, lanes_at(lane0)], from_b[g].at[i, k - 1], peer(bb, k))

    def b_to_c(g, i):
        n, row0, a, bb, c, row_a, row_b = place(g, i)
        for k in (1, 2, 3):
            lands(g, i, 3 + k)
        rows, lane0 = piece_of(row_a, n, at[bb])
        lanes = lanes_at(lane0)
        half[g][1, rows, lanes] = (half[g][1, rows, lanes] + from_b[g][i, 1]) + (from_b[g][i, 0] + from_b[g][i, 2])
        for k in (1, 2, 3):
            copy(g, i, 6 + k, half[g].at[1, rows, lanes], from_c[g].at[i, k - 1], peer(c, k))

    def c_to_b(g, i):
        n, row0, a, bb, c, row_a, row_b = place(g, i)
        for k in (1, 2, 3):
            lands(g, i, 6 + k)
        rows, lane0 = piece_of(row_a, n, at[bb])
        mine = half[g][1, rows, lanes_at(lane0)]
        out = lanes_at(core * 256 + lane0)
        result[g][rows, out] = (mine + from_c[g][i, 1]) + (from_c[g][i, 0] + from_c[g][i, 2])
        for k in (1, 2, 3):
            here = result[g].at[rows, out]
            copy(g, i, 9 + k, here, here, peer(bb, k))

    def b_to_a(g, i):
        n, row0, a, bb, c, row_a, row_b = place(g, i)
        for k in (1, 2, 3):
            lands(g, i, 9 + k)
        here = result[g].at[pl.ds(row_a, n // 4), lanes_at(core * 256, 256)]
        for k in (2, 1, 3):
            copy(g, i, 12 + k, here, here, peer(a, k))
        copy(g, i, 20, here, here, partner)

    def a_to_core(g):
        for k in (1, 3, 2):
            for i in range(3):
                lands(g, i, 12 + k)
                here = result[g].at[chunk(g, i, 4 - k), lanes_at(core * 256, 256)]
                copy(g, i, 20 + k, here, here, partner)

    def finish(g):
        for i in range(3):
            for k in range(4):
                lands(g, i, 20 + k)

    def whole_chunk(g, i):
        row_a = place(g, i)[5]
        return half[g].at[1, pl.ds(row_a, PARTS[g][i] // 4)]

    def exchange(g, i, first, came_from, axis):
        here = whole_chunk(g, i)
        for k in (2, 1, 3):
            copy(g, i, first + k, here, came_from[g].at[i, k - 1], peer(axis, k))

    def a_to_b_whole(g, i):
        for k in (1, 2, 3):
            lands(g, i, k)
        here = whole_chunk(g, i)
        here[...] = (here[...] + from_a[g][i, 1]) + (from_a[g][i, 0] + from_a[g][i, 2])
        exchange(g, i, 3, from_b, ORDERS[i][1])

    def b_to_c_whole(g, i):
        for k in (1, 2, 3):
            lands(g, i, 3 + k)
            flying[g, i, 3 + k].wait_send()
            done.append(flying[g, i, 3 + k])
        here = whole_chunk(g, i)
        here[...] = (here[...] + from_b[g][i, 1]) + (from_b[g][i, 0] + from_b[g][i, 2])
        exchange(g, i, 6, from_c, ORDERS[i][2])

    def c_to_a_whole(g, i):
        for k in (1, 2, 3):
            lands(g, i, 6 + k)
        n, row0, a, bb, c, row_a, row_b = place(g, i)
        out = result[g].at[pl.ds(row_a, n // 4), lanes_at(core * 256, 256)]
        here = whole_chunk(g, i)
        out[...] = (here[...] + from_c[g][i, 1]) + (from_c[g][i, 0] + from_c[g][i, 2])
        for k in (2, 1, 3):
            copy(g, i, 12 + k, out, out, peer(a, k))
        copy(g, i, 20, out, out, partner)

    def step(g, f):
        for i in range(3):
            f(g, i)

    def gradient(l, h):
        rows = pl.ds(pl.multiple_of(h * 256, 256), 256)
        return mm3((xh[l], xl[l]), (dh[l, rows], dl[l, rows]), NT)

    lat2_t = lat_t
    scaled = oc[...] * env_t
    delta_t = keep_d(1, 1, scaled * sp[2] + dlat[2] * (spp[2] * update_t[1]))
    h1[0] = gradient(1, 1 - core)
    start_core(0)
    h1[1] = gradient(1, core)

    dlat_t = scaled
    env_rows = [None, None]
    for l in (1, 0):
        if l == 0:
            delta_t = keep_d(0, 1, dlat_t * sp[1] + dlat[1] * (spp[1] * update_t[0]))
            core_to_a(0)
            h2[0] = gradient(0, 1 - core)
            start_core(1)
            h2[1] = gradient(0, core)
        d_inv_t = mm3((latN[l, 0, H:], latN[l, 1, H:]), delta_t)
        d_inv3, d_t, d_w, d_u = kept[l]
        t_t, pr_t = kept_t[l]
        d_inv3_t = jnp.concatenate([d_inv_t] * 3, axis=0)
        d_t_t = d_inv3_t * pp[l] + d_inv3 * pr_t + with_same(d_inv3_t * tt[l] + d_inv3 * t_t)
        ones = jnp.ones((M, E), F32)
        d_w_t = dotted(outer(dir_t, ones), d_t) + dotted(outer(direction, ones), d_t_t)
        d_u_t = split(d_w_t * env + d_w * env_t)
        env_rows[l] = (jnp.concatenate([d_u[0], d_u_t[0]], axis=1), jnp.concatenate([d_u[1], d_u_t[1]], axis=1))
        back = mm3((latN[l, 0, 0:H], latN[l, 1, 0:H]), delta_t) + mm3((envN[l, 0], envN[l, 1]), padded2(d_u_t))
        dlat_t = dlat_t + back
    core_to_a(1)
    keep_d(2, 1, dlat_t * sp[0] + dlat[0] * (spp[0] * first_t))
    feats2 = split(jnp.concatenate([feats_t, feats], axis=1))
    out_sum = split(lat2_t * env + lat[2] * env_t)
    osum[0], osum[1] = out_sum
    ones = jnp.ones((16, E), BF16)

    def rest(h, slot):
        rows = pl.ds(pl.multiple_of(h * 256, 256), 256)
        for l in (1, 0):
            h3[slot, 64 - 64 * l : 128 - 64 * l] = mm3(env_rows[l], (xh[l, rows], xl[l, rows]), NT)
        h3[slot, 128:160] = mm3(feats2, (dh[2, rows], dl[2, rows]), NT)
        o = dot(ones, osum[0, rows], NT) + dot(ones, osum[1, rows], NT)
        h3[slot, 152:160] = o[0:8]
        h3[slot, 160:192] = jnp.zeros((32, 256), F32)

    rest(1 - core, 0)
    start_core(2)
    rest(core, 1)
    step(0, a_to_b)
    core_to_a(2)
    step(1, a_to_b_whole)
    step(0, b_to_c)
    step(2, a_to_b_whole)
    step(1, b_to_c_whole)
    step(0, c_to_b)
    step(2, b_to_c_whole)
    settled = len(sends)
    step(1, c_to_a_whole)
    step(0, b_to_a)
    step(2, c_to_a_whole)
    for c in sends[:settled]:
        if not any(c is d for d in done):
            c.wait_send()
            done.append(c)
    a_to_core(1)
    a_to_core(0)
    a_to_core(2)
    for g in range(3):
        finish(g)
    for c in sends:
        if not any(c is d for d in done):
            c.wait_send()


def unpack(f_ref, g1_ref, g2_ref, g3_ref, forces_ref, rad_ref, cem_ref, nem_ref, env_ref, lat_ref, out_ref):
    lat_ref[1] = g1_ref[...]
    lat_ref[0] = g2_ref[...]
    env_ref[1] = g3_ref[0:64]
    env_ref[0] = g3_ref[64:128]
    rad_ref[...] = g3_ref[128:136]
    cem_ref[...] = g3_ref[136:141]
    nem_ref[...] = g3_ref[144:149]
    out_ref[...] = g3_ref[152:153]
    forces_ref[...] = f_ref[...]


def shape(*dims):
    return jax.ShapeDtypeStruct(dims, F32)


def on_device(
    positions, species, export_index, edge_center, edge_neighbor, edge_count, force_target, radial_weight, center_embed,
    neighbor_embed, environment_weight, latent_weight, output_weight,
):
    vmem = pl.BlockSpec(memory_space=VMEM)
    scratch = [
        VMEM((3, 1, 1, ATOMS), F32),
        VMEM((1, 1, ATOMS), jnp.int32),
        VMEM((1, 1, ATOMS), jnp.int32),
        VMEM((1, 1, E), jnp.int32),
        VMEM((1, 1, E), jnp.int32),
        VMEM((3, 1, 1, ATOMS), F32),
        VMEM((8, H), F32),
        VMEM((5, H), F32),
        VMEM((5, H), F32),
        VMEM((1, H), F32),
        VMEM((2, 576, 512), F32),
        VMEM((2, 64, 512), F32),
        VMEM((2, 2, 512, 640), BF16),
        VMEM((2, 2, 576, 512), BF16),
        VMEM((2, 2, 64, 512), BF16),
        VMEM((2, 2, 512, 128), BF16),
        VMEM((32, 512), F32),
        VMEM((H, E), F32),
        VMEM((10, 8, 128), F32),
        VMEM((10, 8, 128), F32),
        VMEM((2, 8, 128), F32),
        VMEM((9, 8, 128), F32),
        VMEM((9, 8, 128), F32),
        VMEM((3, H, E), F32),
        VMEM((2, 576, 512), BF16),
        VMEM((2, 576, 512), BF16),
        VMEM((3, 512, 512), BF16),
        VMEM((3, 512, 512), BF16),
        VMEM((3, H, E), F32),
        VMEM((3, H, E), F32),
        VMEM((3, H, E), F32),
        VMEM((2, H, E), BF16),
        VMEM((2, 3 * M, E), F32),
        VMEM((2, 3 * M, E), F32),
        VMEM((2, M, E), F32),
    ]
    for n in ROWS:
        scratch.append(VMEM((2, n, 256), F32))
    for n in ROWS:
        scratch.append(VMEM((n, 256), F32))
    for n in PARTS:
        scratch.append(VMEM((3, 3, n[0] // 4, 256), F32))
    for _ in (1, 2):
        for g, n in enumerate(PARTS):
            scratch.append(VMEM((3, 3) + ((n[0] // 4, 256) if g in (1, 2) else (n[0] // 8, 128)), F32))
    scratch += [
        pltpu.SemaphoreType.DMA((12,)),
        pltpu.SemaphoreType.DMA((3, 8)),
        pltpu.SemaphoreType.DMA((3, 8)),
        pltpu.SemaphoreType.DMA((3, 3, 24)),
        pltpu.SemaphoreType.DMA((3, 3, 24)),
    ]
    any_space = pl.BlockSpec(memory_space=pl.ANY)
    parts = pl.pallas_call(
        kernel,
        out_shape=(VMEM((3, 1, 1, ATOMS), F32),) + tuple(VMEM((n, 512), F32) for n in ROWS),
        in_specs=[any_space] * 5 + [vmem] + [any_space] * 7,
        out_specs=(vmem,) * 4,
        scratch_shapes=scratch,
        compiler_params=pltpu.CompilerParams(collective_id=0, has_side_effects=True, vmem_limit_bytes=56 << 20),
        name="step",
    )(
        positions, species, export_index, edge_center, edge_neighbor, edge_count, force_target, radial_weight, center_embed,
        neighbor_embed, output_weight.reshape(1, 512), jnp.swapaxes(environment_weight, 1, 2), latent_weight,
    )
    outs = pl.pallas_call(
        unpack,
        out_shape=(shape(3, 1, 1, ATOMS), shape(8, 512), shape(5, 512), shape(5, 512), shape(2, 64, 512), shape(2, 576, 512), shape(1, 512)),
        in_specs=[vmem] * 4,
        out_specs=(vmem,) * 7,
        compiler_params=pltpu.CompilerParams(vmem_limit_bytes=32 << 20),
        name="unpack",
    )(*parts)
    forces, radial, near, far, environment, latent, output = outs
    return forces, radial, near, far, jnp.swapaxes(environment, 1, 2), latent, output.reshape(512)


def solution(mesh):
    return jax.shard_map(
        on_device,
        mesh=mesh,
        in_specs=(
            P(None, "slab", "brick", None),
            P("slab", "brick", None),
            P("slab", "brick", None),
            P("slab", "brick", None),
            P("slab", "brick", None),
            P("slab", "brick"),
            P(None, "slab", "brick", None),
            P(),
            P(),
            P(),
            P(),
            P(),
            P(),
        ),
        out_specs=(P(None, "slab", "brick", None), P(), P(), P(), P(), P(), P()),
        check_vma=False,
    )
```

```python
import math

import jax
import jax.numpy as jnp
from jax import lax
from jax.experimental import pallas as pl
from jax.experimental.pallas import tpu as pltpu
from jax.sharding import PartitionSpec as P

F32 = jnp.float32
BF16 = jnp.bfloat16
MESH = pl.DeviceIdType.MESH
VMEM = pltpu.VMEM
NN = (((1,), (0,)), ((), ()))
NT = (((1,), (1,)), ((), ()))
TN = (((0,), (0,)), ((), ()))

cell_width = 1.75
cutoff_radius = 6.0
softening = 0.25

N_SLAB, N_BRICK = 4, 32
H, M, E, ATOMS = 512, 64, 256, 128
ROWS = (576, 576, 192)
PARTS = tuple((n // 3,) * 3 for n in ROWS)
ORDERS = (("x", "y", "z"), ("y", "z", "x"), ("z", "x", "y"))
NEIGHBOURS = [(p, q) for q in (0, 2, 1) for p in (0, 2, 1) if (p, q) != (1, 1)]


def dot(a, b, dims=NN):
    return lax.dot_general(a, b, dims, preferred_element_type=F32)


def split(x):
    high = x.astype(BF16)
    return high, (x - high.astype(F32)).astype(BF16)


def mm3(a, b, dims=NN):
    return dot(a[0], b[0], dims) + (dot(a[0], b[1], dims) + dot(a[1], b[0], dims))


def mm2(a, exact, dims=NN):
    return dot(a[0], exact, dims) + dot(a[1], exact, dims)


def pieces(x):
    a = x.astype(BF16).astype(F32)
    b = (x - a).astype(BF16).astype(F32)
    c = (x - a) - b
    return jnp.concatenate([a, b, c, jnp.zeros_like(x)], axis=0).astype(BF16)


def select(x, hot, dims=NN):
    r = dot(pieces(x), hot, dims)
    return (r[0:8] + r[8:16]) + r[16:24]


def onehot(values, count):
    ids = lax.broadcasted_iota(jnp.int32, (count, values.shape[1]), 0)
    return jnp.where(ids == values, 1.0, 0.0).astype(BF16)


def padded(x):
    return jnp.concatenate([x, jnp.zeros((M, x.shape[1]), x.dtype)], axis=0)


def padded2(x):
    return padded(x[0]), padded(x[1])


def sigmoid(x):
    return 0.5 + 0.5 * jnp.tanh(0.5 * x)


def device_at(core, x, y, z):
    return (lax.rem(x, 2) * 2 + core, (z * 4 + y) * 2 + lax.div(x, 2))


def kernel(
    pos_in, spec_in, exp_in, cen_in, nbr_in, cnt_ref, tgt_in, rad_in, cem_in, nem_in, ow_in, env_hbm, lat_hbm,
    forces_ref, g1_ref, g2_ref, g3_ref,
    pos_ref, spec_ref, exp_ref, cen_ref, nbr_ref, tgt_ref, rad_ref, cem_ref, nem_ref, ow_ref,
    w_lat, w_env, latT, latN, envT, envN, a0, oc,
    tbl, ttbl, sendbuf, gsend, grecv,
    lat, xh, xl, dh, dl, sp, spp, dlat, osum, tt, pp, uu,
    h1, h2, h3, c1, c2, c3, ra1, ra2, ra3, rb1, rb2, rb3, rc1, rc2, rc3,
    wsem, hs, hr, ars, arr,
):
    s, b = lax.axis_index("slab"), lax.axis_index("brick")
    core, x = lax.rem(s, 2), 2 * lax.rem(b, 2) + lax.div(s, 2)
    y, z = lax.rem(lax.div(b, 2), 4), lax.div(b, 8)
    at = {"x": x, "y": y, "z": z}
    partner = device_at(1 - core, x, y, z)

    def peer(axis, k):
        c = dict(at)
        c[axis] = lax.rem(c[axis] + k, 4)
        return device_at(core, c["x"], c["y"], c["z"])

    def around(p, q):
        return (lax.rem(s + p + N_SLAB - 1, N_SLAB), lax.rem(b + q + N_BRICK - 1, N_BRICK))

    barrier = pltpu.get_barrier_semaphore()
    everyone = [around(p, q) for p, q in NEIGHBOURS] + [partner] + [peer(a, k) for a in "xyz" for k in (1, 2, 3)]
    for d in everyone:
        pl.semaphore_signal(barrier, inc=1, device_id=d, device_id_type=MESH)

    loads = [
        pltpu.make_async_copy(env_hbm, w_env, wsem.at[0]),
        pltpu.make_async_copy(lat_hbm, w_lat, wsem.at[1]),
    ]
    firsts = [
        pltpu.make_async_copy(pos_in, pos_ref, wsem.at[2]),
        pltpu.make_async_copy(spec_in, spec_ref, wsem.at[3]),
        pltpu.make_async_copy(exp_in, exp_ref, wsem.at[4]),
    ]
    loads += [
        pltpu.make_async_copy(cen_in, cen_ref, wsem.at[5]),
        pltpu.make_async_copy(nbr_in, nbr_ref, wsem.at[6]),
        pltpu.make_async_copy(tgt_in, tgt_ref, wsem.at[7]),
        pltpu.make_async_copy(rad_in, rad_ref, wsem.at[8]),
        pltpu.make_async_copy(cem_in, cem_ref, wsem.at[9]),
        pltpu.make_async_copy(nem_in, nem_ref, wsem.at[10]),
        pltpu.make_async_copy(ow_in, ow_ref, wsem.at[11]),
    ]
    for c in firsts + loads:
        c.start()
    for c in firsts:
        c.wait()

    tbl[0] = jnp.zeros((8, ATOMS), F32)
    for m in range(3):
        tbl[0, m : m + 1, :] = pos_ref[m, 0]
    tbl[0, 3:4, :] = spec_ref[0].astype(F32)
    hot_exp = onehot(exp_ref[0], ATOMS)
    sendbuf[0] = select(tbl[0], hot_exp)

    pl.semaphore_wait(barrier, len(everyone))

    def halo(stage, sources, lands, back):
        out = []
        for i, (p, q) in enumerate(NEIGHBOURS):
            k = 3 * p + q
            to = around(p, q) if back else around(2 - p, 2 - q)
            out.append(
                pltpu.make_async_remote_copy(
                    src_ref=sources(k), dst_ref=lands(k), send_sem=hs.at[stage, i], recv_sem=hr.at[stage, i],
                    device_id=to, device_id_type=MESH,
                )
            )
        for c in out:
            c.start()
        return out

    sends = []
    first = halo(0, lambda k: sendbuf.at[0], lambda k: tbl.at[1 + k], False)
    sends += first

    tbl[5] = sendbuf[0]
    for c in loads:
        c.wait()
    center = cen_ref[0]
    hot_c = onehot(center, ATOMS)
    hot_n = onehot(nbr_ref[0], 10 * ATOMS)
    same = dot(hot_c, hot_c, TN).astype(BF16)
    lane = lax.broadcasted_iota(jnp.int32, (1, E), 1)
    live = jnp.where(lane < cnt_ref[...], 1.0, 0.0)
    o_col = jnp.transpose(jnp.broadcast_to(ow_ref[...], (128, H)))
    oc[...] = jnp.concatenate([o_col, o_col], axis=1)
    a0[...] = jnp.zeros_like(a0)
    a0[0:8] = rad_ref[...]
    a0[8:13] = cem_ref[...]
    a0[16:21] = nem_ref[...]
    a0s = split(a0[...])
    for l in range(2):
        w = w_lat[l]
        latN[l, 0], latN[l, 1] = split(w)
        latT[l, 0], latT[l, 1] = split(jnp.transpose(padded(w)))
        w = w_env[l]
        envT[l, 0], envT[l, 1] = split(w)
        envN[l, 0], envN[l, 1] = split(jnp.transpose(padded(w)))

    pc = select(tbl[0], hot_c)

    for c in first:
        c.wait_recv()

    row = lax.broadcasted_iota(jnp.int32, (8, 1), 0)
    blocks = [tbl[0]]
    for p in range(3):
        for q in range(3):
            t = tbl[1 + 3 * p + q]
            if (p, q) != (1, 1):
                cross_z = (lax.div(s + p - 1 + N_SLAB, N_SLAB) - 1).astype(F32) * (N_SLAB * cell_width)
                cross_y = (lax.div(b + q - 1 + N_BRICK, N_BRICK) - 1).astype(F32) * (N_BRICK * cell_width)
                t = t + jnp.where(row == 2, cross_z, 0.0) + jnp.where(row == 1, cross_y, 0.0)
            blocks.append(t)
    pn = select(jnp.concatenate(blocks, axis=1), hot_n)
    vec = jnp.where(row < 3, pn - pc, 0.0)
    squared = jnp.sum(vec * vec, axis=0, keepdims=True) + softening
    dist = jnp.sqrt(squared)
    inv_d = 1.0 / dist
    base = 1.0 - squared / (cutoff_radius * cutoff_radius)
    env = base * base * live
    direction = vec * inv_d
    order = (row + 1).astype(F32) * (math.pi / cutoff_radius)
    angle = order * dist
    sine, cosine = jnp.sin(angle), jnp.cos(angle)
    basis = sine * inv_d
    basis_d = (order * cosine - basis) * inv_d
    hot_sc = jnp.where(row.astype(F32) == pc[3:4], 1.0, 0.0)
    hot_sn = jnp.where(row.astype(F32) == pn[3:4], 1.0, 0.0)
    feats = jnp.concatenate([basis, hot_sc, hot_sn, jnp.zeros((8, E), F32)], axis=0)

    def activation(i, value):
        g = sigmoid(value)
        sp[i] = g * (1.0 + value * (1.0 - g))
        spp[i] = value
        return value * g

    def second_derivative(i):
        value = spp[i]
        g = sigmoid(value)
        spp[i] = (g * (1.0 - g)) * (2.0 + value * (1.0 - 2.0 * g))

    def keep_x(l, half, rows, value):
        high, low = split(value)
        lanes = slice(E * half, E * half + E)
        xh[l, rows, lanes] = high
        xl[l, rows, lanes] = low
        return high, low

    def keep_d(l, half, value):
        high, low = split(value)
        lanes = slice(E * half, E * half + E)
        dh[l, :, lanes] = high
        dl[l, :, lanes] = low
        return high, low

    def thirds(v):
        return [v[m * M : m * M + M] for m in range(3)]

    def outer(d, w):
        return jnp.concatenate([d[m : m + 1] * w for m in range(3)], axis=0)

    def with_same(t):
        return mm2(split(t), same)

    def dotted(a, c):
        r = a * c
        return (r[0:M] + r[M : 2 * M]) + r[2 * M :]

    lat[0] = activation(0, mm3(a0s, split(feats), TN))
    for l in range(2):
        now = keep_x(l, 1, slice(0, H), lat[l])
        u = mm3((envT[l, 0], envT[l, 1]), now)
        uu[l] = u
        t = outer(direction, u * env)
        tt[l] = t
        pr = with_same(t)
        pp[l] = pr
        inv = keep_x(l, 1, slice(H, H + M), dotted(t, pr))
        update = mm3((latT[l, 0, :, 0:H], latT[l, 1, :, 0:H]), now) + mm3((latT[l, 0, :, H:], latT[l, 1, :, H:]), padded2(inv))
        lat[l + 1] = lat[l] + activation(l + 1, update)

    d_env = jnp.sum(oc[...] * lat[2], axis=0, keepdims=True)
    d_dir = [jnp.zeros((1, E), F32) for _ in range(3)]
    dlat[2] = oc[...] * env
    kept = [None, None]
    for l in (1, 0):
        delta = keep_d(l, 0, dlat[l + 1] * sp[l + 1])
        d_inv = mm3((latN[l, 0, H:], latN[l, 1, H:]), delta)
        d_inv3 = jnp.concatenate([d_inv] * 3, axis=0)
        d_t = d_inv3 * pp[l] + with_same(d_inv3 * tt[l])
        w = uu[l] * env
        d_w = dotted(outer(direction, jnp.ones((M, E), F32)), d_t)
        for m, part in enumerate(thirds(d_t)):
            d_dir[m] += jnp.sum(part * w, axis=0, keepdims=True)
        d_env += jnp.sum(d_w * uu[l], axis=0, keepdims=True)
        d_u = split(d_w * env)
        kept[l] = (d_inv3, d_t, d_w, d_u)
        back = mm3((latN[l, 0, 0:H], latN[l, 1, 0:H]), delta) + mm3((envN[l, 0], envN[l, 1]), padded2(d_u))
        dlat[l] = dlat[l + 1] + back
    delta0 = keep_d(2, 0, dlat[0] * sp[0])
    d_basis = mm3(a0s, delta0)[0:8]
    d_dir8 = jnp.concatenate(d_dir + [jnp.zeros((5, E), F32)], axis=0)
    d_dist = jnp.sum(d_basis * basis_d, axis=0, keepdims=True) - jnp.sum(d_dir8 * direction, axis=0, keepdims=True) * inv_d
    base_d = (-2.0 / (cutoff_radius * cutoff_radius)) * base * live
    d_squared = d_env * base_d + d_dist * (0.5 * inv_d)
    d_vec = d_dir8 * inv_d + 2.0 * vec * d_squared
    d_table = select(d_vec, hot_n, NT)
    own = d_table[:, 0:ATOMS] - select(d_vec, hot_c, NT)
    for k in range(9):
        gsend[k] = d_table[:, ATOMS * (k + 1) : ATOMS * (k + 2)]
    second = halo(1, lambda k: gsend.at[k], lambda k: grecv.at[k], True)
    sends += second
    second_derivative(0)
    second_derivative(1)
    for c in second:
        c.wait_recv()
    returned = gsend[4]
    for p, q in NEIGHBOURS:
        returned = returned + grecv[3 * p + q]
    total = own + select(returned, hot_exp, NT)
    ttbl[0] = jnp.zeros((8, ATOMS), F32)
    for m in range(3):
        forces_ref[m, 0] = -total[m : m + 1]
        ttbl[0, m : m + 1, :] = (2.0 / (3.0 * ATOMS)) * (total[m : m + 1] + tgt_ref[m, 0])

    sendbuf[1] = select(ttbl[0], hot_exp)
    third = halo(2, lambda k: sendbuf.at[1], lambda k: ttbl.at[1 + k], False)
    sends += third
    ttbl[5] = sendbuf[1]
    second_derivative(2)
    vc = select(ttbl[0], hot_c)
    for c in third:
        c.wait_recv()
    vn = select(jnp.concatenate([ttbl[k] for k in range(10)], axis=1), hot_n)
    vec_t = vn - vc
    dist_t = jnp.sum(vec * vec_t, axis=0, keepdims=True) * inv_d
    env_t = (2.0 * base_d) * (dist * dist_t)
    dir_t = (vec_t - direction * dist_t) * inv_d
    basis_t = basis_d * dist_t
    feats_t = jnp.concatenate([basis_t, jnp.zeros((24, E), F32)], axis=0)

    first_t = mm3(a0s, split(feats_t), TN)
    lat_t = sp[0] * first_t
    kept_t = [None, None]
    update_t = [None, None]
    for l in range(2):
        now = keep_x(l, 0, slice(0, H), lat_t)
        u_t = mm3((envT[l, 0], envT[l, 1]), now)
        w = uu[l] * env
        w_t = u_t * env + uu[l] * env_t
        t_t = outer(dir_t, w) + outer(direction, w_t)
        pr_t = with_same(t_t)
        inv_t = keep_x(l, 0, slice(H, H + M), dotted(t_t, pp[l]) + dotted(tt[l], pr_t))
        kept_t[l] = (t_t, pr_t)
        update_t[l] = mm3((latT[l, 0, :, 0:H], latT[l, 1, :, 0:H]), now) + mm3((latT[l, 0, :, H:], latT[l, 1, :, H:]), padded2(inv_t))
        lat_t = lat_t + sp[l + 1] * update_t[l]

    half = (h1, h2, h3)
    from_core = (c1, c2, c3)
    from_a, from_b, from_c = (ra1, ra2, ra3), (rb1, rb2, rb3), (rc1, rc2, rc3)
    result = (g1_ref, g2_ref, g3_ref)
    flying, done = {}, []

    def place(g, i):
        n = PARTS[g][i]
        row0 = sum(PARTS[g][:i])
        a, bb, c = ORDERS[i]
        row_a = row0 + at[a] * (n // 4)
        row_b = row_a + lax.div(at[bb], 2) * (n // 8)
        return n, row0, a, bb, c, pl.multiple_of(row_a, 8), pl.multiple_of(row_b, 8)

    def piece_of(row_a, n, where):
        rows = pl.ds(pl.multiple_of(row_a + lax.div(where, 2) * (n // 8), 8), n // 8)
        return rows, lax.rem(where, 2) * 128

    def copy(g, i, j, src, dst, to):
        c = pltpu.make_async_remote_copy(
            src_ref=src, dst_ref=dst, send_sem=ars.at[g, i, j], recv_sem=arr.at[g, i, j], device_id=to, device_id_type=MESH
        )
        c.start()
        sends.append(c)
        flying[g, i, j] = c

    def lands(g, i, j):
        flying[g, i, j].wait_recv()

    def lanes_at(first, count=128):
        return pl.ds(pl.multiple_of(first, 128), count)

    def chunk(g, i, k):
        n, row0, a, *_ = place(g, i)
        return pl.ds(pl.multiple_of(row0 + lax.rem(at[a] + k, 4) * (n // 4), 8), n // 4)

    def start_core(g):
        for k in (2, 1, 3, 0):
            for i in range(3):
                rows = chunk(g, i, k)
                copy(g, i, 16 + k, half[g].at[0, rows], from_core[g].at[rows], partner)

    def core_to_a(g):
        for k in (2, 1, 3, 0):
            for i in range(3):
                lands(g, i, 16 + k)
                rows = chunk(g, i, k)
                half[g][1, rows] = half[g][1, rows] + from_core[g][rows]
                if k:
                    a = ORDERS[i][0]
                    copy(g, i, k, half[g].at[1, rows], from_a[g].at[i, k - 1], peer(a, k))

    def a_to_b(g, i):
        n, row0, a, bb, c, row_a, row_b = place(g, i)
        for k in (1, 2, 3):
            lands(g, i, k)
        rows = pl.ds(row_a, n // 4)
        half[g][1, rows] = (half[g][1, rows] + from_a[g][i, 1]) + (from_a[g][i, 0] + from_a[g][i, 2])
        for k in (1, 2, 3):
            rows, lane0 = piece_of(row_a, n, lax.rem(at[bb] + k, 4))
            copy(g, i, 3 + k, half[g].at[1, rows, lanes_at(lane0)], from_b[g].at[i, k - 1], peer(bb, k))

    def b_to_c(g, i):
        n, row0, a, bb, c, row_a, row_b = place(g, i)
        for k in (1, 2, 3):
            lands(g, i, 3 + k)
        rows, lane0 = piece_of(row_a, n, at[bb])
        lanes = lanes_at(lane0)
        half[g][1, rows, lanes] = (half[g][1, rows, lanes] + from_b[g][i, 1]) + (from_b[g][i, 0] + from_b[g][i, 2])
        for k in (1, 2, 3):
            copy(g, i, 6 + k, half[g].at[1, rows, lanes], from_c[g].at[i, k - 1], peer(c, k))

    def c_to_b(g, i):
        n, row0, a, bb, c, row_a, row_b = place(g, i)
        for k in (1, 2, 3):
            lands(g, i, 6 + k)
        rows, lane0 = piece_of(row_a, n, at[bb])
        mine = half[g][1, rows, lanes_at(lane0)]
        out = lanes_at(core * 256 + lane0)
        result[g][rows, out] = (mine + from_c[g][i, 1]) + (from_c[g][i, 0] + from_c[g][i, 2])
        for k in (1, 2, 3):
            here = result[g].at[rows, out]
            copy(g, i, 9 + k, here, here, peer(bb, k))

    def b_to_a(g, i):
        n, row0, a, bb, c, row_a, row_b = place(g, i)
        for k in (1, 2, 3):
            lands(g, i, 9 + k)
        here = result[g].at[pl.ds(row_a, n // 4), lanes_at(core * 256, 256)]
        for k in (2, 1, 3):
            copy(g, i, 12 + k, here, here, peer(a, k))
        copy(g, i, 20, here, here, partner)

    def a_to_core(g):
        for k in (1, 3, 2):
            for i in range(3):
                lands(g, i, 12 + k)
                here = result[g].at[chunk(g, i, 4 - k), lanes_at(core * 256, 256)]
                copy(g, i, 20 + k, here, here, partner)

    def finish(g):
        for i in range(3):
            for k in range(4):
                lands(g, i, 20 + k)

    def whole_chunk(g, i):
        row_a = place(g, i)[5]
        return half[g].at[1, pl.ds(row_a, PARTS[g][i] // 4)]

    def exchange(g, i, first, came_from, axis):
        here = whole_chunk(g, i)
        for k in (2, 1, 3):
            copy(g, i, first + k, here, came_from[g].at[i, k - 1], peer(axis, k))

    def a_to_b_whole(g, i):
        for k in (1, 2, 3):
            lands(g, i, k)
        here = whole_chunk(g, i)
        here[...] = (here[...] + from_a[g][i, 1]) + (from_a[g][i, 0] + from_a[g][i, 2])
        exchange(g, i, 3, from_b, ORDERS[i][1])

    def b_to_c_whole(g, i):
        for k in (1, 2, 3):
            lands(g, i, 3 + k)
            flying[g, i, 3 + k].wait_send()
            done.append(flying[g, i, 3 + k])
        here = whole_chunk(g, i)
        here[...] = (here[...] + from_b[g][i, 1]) + (from_b[g][i, 0] + from_b[g][i, 2])
        exchange(g, i, 6, from_c, ORDERS[i][2])

    def c_to_a_whole(g, i):
        for k in (1, 2, 3):
            lands(g, i, 6 + k)
        n, row0, a, bb, c, row_a, row_b = place(g, i)
        out = result[g].at[pl.ds(row_a, n // 4), lanes_at(core * 256, 256)]
        here = whole_chunk(g, i)
        out[...] = (here[...] + from_c[g][i, 1]) + (from_c[g][i, 0] + from_c[g][i, 2])
        for k in (2, 1, 3):
            copy(g, i, 12 + k, out, out, peer(a, k))
        copy(g, i, 20, out, out, partner)

    def step(g, f):
        for i in range(3):
            f(g, i)

    def gradient(l, h):
        rows = pl.ds(pl.multiple_of(h * 256, 256), 256)
        return mm3((xh[l], xl[l]), (dh[l, rows], dl[l, rows]), NT)

    lat2_t = lat_t
    scaled = oc[...] * env_t
    delta_t = keep_d(1, 1, scaled * sp[2] + dlat[2] * (spp[2] * update_t[1]))
    h1[0] = gradient(1, 1 - core)
    start_core(0)
    h1[1] = gradient(1, core)

    dlat_t = scaled
    env_rows = [None, None]
    for l in (1, 0):
        if l == 0:
            delta_t = keep_d(0, 1, dlat_t * sp[1] + dlat[1] * (spp[1] * update_t[0]))
            core_to_a(0)
            h2[0] = gradient(0, 1 - core)
            start_core(1)
            h2[1] = gradient(0, core)
        d_inv_t = mm3((latN[l, 0, H:], latN[l, 1, H:]), delta_t)
        d_inv3, d_t, d_w, d_u = kept[l]
        t_t, pr_t = kept_t[l]
        d_inv3_t = jnp.concatenate([d_inv_t] * 3, axis=0)
        d_t_t = d_inv3_t * pp[l] + d_inv3 * pr_t + with_same(d_inv3_t * tt[l] + d_inv3 * t_t)
        ones = jnp.ones((M, E), F32)
        d_w_t = dotted(outer(dir_t, ones), d_t) + dotted(outer(direction, ones), d_t_t)
        d_u_t = split(d_w_t * env + d_w * env_t)
        env_rows[l] = (jnp.concatenate([d_u[0], d_u_t[0]], axis=1), jnp.concatenate([d_u[1], d_u_t[1]], axis=1))
        back = mm3((latN[l, 0, 0:H], latN[l, 1, 0:H]), delta_t) + mm3((envN[l, 0], envN[l, 1]), padded2(d_u_t))
        dlat_t = dlat_t + back
    core_to_a(1)
    keep_d(2, 1, dlat_t * sp[0] + dlat[0] * (spp[0] * first_t))
    feats2 = split(jnp.concatenate([feats_t, feats], axis=1))
    out_sum = split(lat2_t * env + lat[2] * env_t)
    osum[0], osum[1] = out_sum
    ones = jnp.ones((16, E), BF16)

    def rest(h, slot):
        rows = pl.ds(pl.multiple_of(h * 256, 256), 256)
        for l in (1, 0):
            h3[slot, 64 - 64 * l : 128 - 64 * l] = mm3(env_rows[l], (xh[l, rows], xl[l, rows]), NT)
        h3[slot, 128:160] = mm3(feats2, (dh[2, rows], dl[2, rows]), NT)
        o = dot(ones, osum[0, rows], NT) + dot(ones, osum[1, rows], NT)
        h3[slot, 152:160] = o[0:8]
        h3[slot, 160:192] = jnp.zeros((32, 256), F32)

    rest(1 - core, 0)
    start_core(2)
    step(0, a_to_b)
    rest(core, 1)
    core_to_a(2)
    step(1, a_to_b_whole)
    step(0, b_to_c)
    step(2, a_to_b_whole)
    step(1, b_to_c_whole)
    step(0, c_to_b)
    step(2, b_to_c_whole)
    settled = len(sends)
    step(1, c_to_a_whole)
    step(0, b_to_a)
    step(2, c_to_a_whole)
    for c in sends[:settled]:
        if not any(c is d for d in done):
            c.wait_send()
            done.append(c)
    a_to_core(1)
    a_to_core(0)
    a_to_core(2)
    for g in range(3):
        finish(g)
    for c in sends:
        if not any(c is d for d in done):
            c.wait_send()


def unpack(f_ref, g1_ref, g2_ref, g3_ref, forces_ref, rad_ref, cem_ref, nem_ref, env_ref, lat_ref, out_ref):
    lat_ref[1] = g1_ref[...]
    lat_ref[0] = g2_ref[...]
    env_ref[1] = g3_ref[0:64]
    env_ref[0] = g3_ref[64:128]
    rad_ref[...] = g3_ref[128:136]
    cem_ref[...] = g3_ref[136:141]
    nem_ref[...] = g3_ref[144:149]
    out_ref[...] = g3_ref[152:153]
    forces_ref[...] = f_ref[...]


def shape(*dims):
    return jax.ShapeDtypeStruct(dims, F32)


def on_device(
    positions, species, export_index, edge_center, edge_neighbor, edge_count, force_target, radial_weight, center_embed,
    neighbor_embed, environment_weight, latent_weight, output_weight,
):
    vmem = pl.BlockSpec(memory_space=VMEM)
    scratch = [
        VMEM((3, 1, 1, ATOMS), F32),
        VMEM((1, 1, ATOMS), jnp.int32),
        VMEM((1, 1, ATOMS), jnp.int32),
        VMEM((1, 1, E), jnp.int32),
        VMEM((1, 1, E), jnp.int32),
        VMEM((3, 1, 1, ATOMS), F32),
        VMEM((8, H), F32),
        VMEM((5, H), F32),
        VMEM((5, H), F32),
        VMEM((1, H), F32),
        VMEM((2, 576, 512), F32),
        VMEM((2, 64, 512), F32),
        VMEM((2, 2, 512, 640), BF16),
        VMEM((2, 2, 576, 512), BF16),
        VMEM((2, 2, 64, 512), BF16),
        VMEM((2, 2, 512, 128), BF16),
        VMEM((32, 512), F32),
        VMEM((H, E), F32),
        VMEM((10, 8, 128), F32),
        VMEM((10, 8, 128), F32),
        VMEM((2, 8, 128), F32),
        VMEM((9, 8, 128), F32),
        VMEM((9, 8, 128), F32),
        VMEM((3, H, E), F32),
        VMEM((2, 576, 512), BF16),
        VMEM((2, 576, 512), BF16),
        VMEM((3, 512, 512), BF16),
        VMEM((3, 512, 512), BF16),
        VMEM((3, H, E), F32),
        VMEM((3, H, E), F32),
        VMEM((3, H, E), F32),
        VMEM((2, H, E), BF16),
        VMEM((2, 3 * M, E), F32),
        VMEM((2, 3 * M, E), F32),
        VMEM((2, M, E), F32),
    ]
    for n in ROWS:
        scratch.append(VMEM((2, n, 256), F32))
    for n in ROWS:
        scratch.append(VMEM((n, 256), F32))
    for n in PARTS:
        scratch.append(VMEM((3, 3, n[0] // 4, 256), F32))
    for _ in (1, 2):
        for g, n in enumerate(PARTS):
            scratch.append(VMEM((3, 3) + ((n[0] // 4, 256) if g in (1, 2) else (n[0] // 8, 128)), F32))
    scratch += [
        pltpu.SemaphoreType.DMA((12,)),
        pltpu.SemaphoreType.DMA((3, 8)),
        pltpu.SemaphoreType.DMA((3, 8)),
        pltpu.SemaphoreType.DMA((3, 3, 24)),
        pltpu.SemaphoreType.DMA((3, 3, 24)),
    ]
    any_space = pl.BlockSpec(memory_space=pl.ANY)
    parts = pl.pallas_call(
        kernel,
        out_shape=(VMEM((3, 1, 1, ATOMS), F32),) + tuple(VMEM((n, 512), F32) for n in ROWS),
        in_specs=[any_space] * 5 + [vmem] + [any_space] * 7,
        out_specs=(vmem,) * 4,
        scratch_shapes=scratch,
        compiler_params=pltpu.CompilerParams(collective_id=0, has_side_effects=True, vmem_limit_bytes=56 << 20),
        name="step",
    )(
        positions, species, export_index, edge_center, edge_neighbor, edge_count, force_target, radial_weight, center_embed,
        neighbor_embed, output_weight.reshape(1, 512), jnp.swapaxes(environment_weight, 1, 2), latent_weight,
    )
    outs = pl.pallas_call(
        unpack,
        out_shape=(shape(3, 1, 1, ATOMS), shape(8, 512), shape(5, 512), shape(5, 512), shape(2, 64, 512), shape(2, 576, 512), shape(1, 512)),
        in_specs=[vmem] * 4,
        out_specs=(vmem,) * 7,
        compiler_params=pltpu.CompilerParams(vmem_limit_bytes=32 << 20),
        name="unpack",
    )(*parts)
    forces, radial, near, far, environment, latent, output = outs
    return forces, radial, near, far, jnp.swapaxes(environment, 1, 2), latent, output.reshape(512)


def solution(mesh):
    return jax.shard_map(
        on_device,
        mesh=mesh,
        in_specs=(
            P(None, "slab", "brick", None),
            P("slab", "brick", None),
            P("slab", "brick", None),
            P("slab", "brick", None),
            P("slab", "brick", None),
            P("slab", "brick"),
            P(None, "slab", "brick", None),
            P(),
            P(),
            P(),
            P(),
            P(),
            P(),
        ),
        out_specs=(P(None, "slab", "brick", None), P(), P(), P(), P(), P(), P()),
        check_vma=False,
    )
```
